1024 devices in a mesh: lon: 64 (over y, x, z_hi), lat: 16 (over z_lo, core).
Axes of the slice: x: 4, y: 4, z: 32 (z_hi: 4, z_lo: 8; z = z_hi * 8 + z_lo), core: 2. Of those that a mesh axis runs over, the one named last changes fastest.
Arguments:
- thermal_tracer: float32 [6, 512, 8192], P(None, 'lat', 'lon'), may hold values from -6 to 6
- saltiness_tracer: float32 [6, 512, 8192], P(None, 'lat', 'lon'), may hold values from -6 to 6
- eastward_transport: float32 [6, 512, 8192], P(None, 'lat', 'lon'), may hold values from -3 to 3
- northward_transport: float32 [6, 512, 8192], P(None, 'lat', 'lon'), may hold values from -3 to 3
- eastward_spacing: float32 [512, 8192], P('lat', 'lon'), may hold values from 0.25 to 1.75
- southward_spacing: float32 [512, 8192], P('lat', 'lon'), may hold values from 0.25 to 1.75
- ocean_layer_depth: int32 [512, 8192], P('lat', 'lon'), may hold values from 0 to 6
Outputs:
- new_temperature: float32 [6, 512, 8192], P(None, 'lat', 'lon')
- new_salinity: float32 [6, 512, 8192], P(None, 'lat', 'lon')
The draws below stay inside these ranges and needn't reach their ends.
Inputs may be any that keep to these rules, and one draw needn't show every extreme that they name: ocean_layer_depth[j, i] counts the wet levels of column (j, i); 0 marks land.
All inputs are finite; a program needn't handle non-finite values.
Results may differ from the reference program's by a relative error of at most 0.0003.
Values sent between devices are 32-bit elements; how exact they have to be, the bound alone decides.
A program may use at most 32 MiB of HBM per device.

```python
import jax
import jax.numpy as jnp
from jax import lax

DEPTH_LAYERS = 6
PARALLEL_NUM = 512
MERIDIAN_NUM = 8192
N_LAT = 16


def place_ends(drawn, stream_key, smallest, top_value):
    shape = drawn.shape
    spot = [jax.random.randint(jax.random.fold_in(stream_key, axis), (), 0, shape[axis]) for axis in range(len(shape))]
    drawn = drawn.at[tuple(spot)].set(smallest)
    longest = shape.index(max(shape))
    spot[longest] = (spot[longest] + 1) % shape[longest]
    return drawn.at[tuple(spot)].set(top_value)


def shard_levels(rng, shape, pieces, least, top_value):
    level, own = 1.0, jax.random.fold_in(rng, 6)
    for dim, blocks in pieces:
        steps = jnp.exp(jax.random.uniform(jax.random.fold_in(own, dim), (blocks,), jnp.float32, least / len(pieces), top_value / len(pieces)))
        level = level * jnp.repeat(steps, shape[dim] // blocks).reshape([-1 if axis == dim else 1 for axis in range(len(shape))])
    return level


def bell_draw(stream_key, shape, width, limit, split=(), held_as=jnp.bfloat16):
    entries = jax.random.normal(stream_key, shape, jnp.float32) * width
    if len(split) > 0:
        entries = shard_levels(stream_key, shape, split, -0.22, 0.18) * entries
    return jnp.clip(entries, min=-limit, max=limit).astype(held_as)


def setup_inputs(seed: int = 0) -> dict:
    arg_keys = jax.random.split(jax.random.key(seed), 8)
    return {
        "thermal_tracer": bell_draw(arg_keys[0], (DEPTH_LAYERS, PARALLEL_NUM, MERIDIAN_NUM), 1.0, 6.0, ((1, 16), (2, 64)), jnp.float32),
        "saltiness_tracer": bell_draw(arg_keys[1], (DEPTH_LAYERS, PARALLEL_NUM, MERIDIAN_NUM), 1.0, 6.0, ((1, 16), (2, 64)), jnp.float32),
        "eastward_transport": bell_draw(arg_keys[2], (DEPTH_LAYERS, PARALLEL_NUM, MERIDIAN_NUM), 0.3, 3.0, ((1, 16), (2, 64)), jnp.float32),
        "northward_transport": bell_draw(arg_keys[3], (DEPTH_LAYERS, PARALLEL_NUM, MERIDIAN_NUM), 0.3, 3.0, ((1, 16), (2, 64)), jnp.float32),
        "eastward_spacing": jnp.clip(1.0 + 0.15 * jax.random.normal(arg_keys[4], (PARALLEL_NUM, MERIDIAN_NUM), jnp.float32), 0.25, 1.75),
        "southward_spacing": jnp.clip(1.0 + 0.15 * jax.random.normal(arg_keys[5], (PARALLEL_NUM, MERIDIAN_NUM), jnp.float32), 0.25, 1.75),
        "ocean_layer_depth": place_ends(jax.random.randint(arg_keys[6], (PARALLEL_NUM, MERIDIAN_NUM), 0, DEPTH_LAYERS + 1), jax.random.fold_in(arg_keys[6], 1), 0, DEPTH_LAYERS).astype(jnp.int32),
    }


TIME_STEP = 0.2
DIFFUSIVITY = 0.5
EXPANSION = 0.2
CONTRACTION = 0.8
STRAT_FLOOR = 0.5
SLOPE_LIMIT = 2.0


def minmod(first_jump, second_jump):
    return 0.5 * (jnp.sign(first_jump) + jnp.sign(second_jump)) * jnp.minimum(jnp.abs(first_jump), jnp.abs(second_jump))


def vertical(tracer):
    upper = jnp.concatenate([tracer[:1], tracer[:-1]], 0)
    lower = jnp.concatenate([tracer[1:], tracer[-1:]], 0)
    return 0.5 * (lower - upper)


def face_flux(tracer, density, tracer_dz, density_dz, speed_all, along_all, across_all, wet):
    inner = tracer.shape[-1] - 4
    face_wet = wet[..., :-1] * wet[..., 1:]
    jumps = (tracer[..., 1:] - tracer[..., :-1]) * face_wet
    density_jumps = (density[..., 1:] - density[..., :-1]) * face_wet
    middle = slice(1, inner + 2)
    length = 0.5 * (along_all[..., 1:inner + 2] + along_all[..., 2:inner + 3])
    breadth = 0.5 * (across_all[..., 1:inner + 2] + across_all[..., 2:inner + 3])
    speed = speed_all[..., middle]
    factor = 0.5 * (1.0 - jnp.abs(speed * TIME_STEP / length))
    left_value = tracer[..., 1:inner + 2] + factor * minmod(jumps[..., 0:inner + 1], jumps[..., middle])
    right_value = tracer[..., 2:inner + 3] - factor * minmod(jumps[..., middle], jumps[..., 2:inner + 3])
    upwind = jnp.where(speed >= 0.0, left_value, right_value)
    advective = breadth * speed * face_wet[..., middle] * upwind
    strat = jnp.maximum(0.5 * (density_dz[..., 1:inner + 2] + density_dz[..., 2:inner + 3]), STRAT_FLOOR)
    slope = jnp.clip(density_jumps[..., middle] / length / strat, -SLOPE_LIMIT, SLOPE_LIMIT)
    gradient_z = 0.5 * (tracer_dz[..., 1:inner + 2] + tracer_dz[..., 2:inner + 3])
    diffusive = -DIFFUSIVITY * breadth * face_wet[..., middle] * (jumps[..., middle] / length - slope * gradient_z)
    return advective + diffusive


def step_block(padded, layer_pile):
    parallel_sum = padded.shape[1] - 4
    meridian_sum = padded.shape[2] - 4
    width_t = padded[4 * layer_pile]
    height_t = padded[4 * layer_pile + 1]
    bottom = padded[4 * layer_pile + 2]
    level_ids = jnp.arange(layer_pile).astype(padded.dtype)
    wet = (level_ids[:, None, None] < bottom[None]).astype(padded.dtype)
    density = (CONTRACTION * padded[layer_pile:2 * layer_pile] - EXPANSION * padded[0:layer_pile]) * wet
    density_dz = vertical(density)
    rows_in = slice(2, parallel_sum + 2)
    cols_in = slice(2, meridian_sum + 2)

    def turned(source):
        return jnp.swapaxes(source[..., cols_in], -1, -2)

    area = (width_t * height_t)[rows_in, cols_in]
    results = []
    for position in range(2):
        tracer = padded[position * layer_pile:(position + 1) * layer_pile] * wet
        tracer_dz = vertical(tracer)
        flux_x = face_flux(tracer[:, rows_in], density[:, rows_in], tracer_dz[:, rows_in], density_dz[:, rows_in],
                           padded[2 * layer_pile:3 * layer_pile, rows_in], width_t[None, rows_in], height_t[None, rows_in],
                           wet[:, rows_in])
        flux_y = jnp.swapaxes(face_flux(turned(tracer), turned(density), turned(tracer_dz), turned(density_dz),
                                        turned(padded[3 * layer_pile:4 * layer_pile]), turned(height_t[None]),
                                        turned(width_t[None]), turned(wet)), -1, -2)
        divergence = (flux_x[..., 1:] - flux_x[..., :-1]) + (flux_y[:, 1:, :] - flux_y[:, :-1, :])
        updated = tracer[:, rows_in, cols_in] - TIME_STEP * divergence / area
        results.append(wet[:, rows_in, cols_in] * updated)
    return results[0], results[1]


def reference(thermal_tracer, saltiness_tracer, eastward_transport, northward_transport, eastward_spacing, southward_spacing, ocean_layer_depth):
    layer_pile = thermal_tracer.shape[0]
    entire_parallels = thermal_tracer.shape[1]
    entire_meridians = thermal_tracer.shape[2]
    block_rows = entire_parallels // N_LAT
    bottom_float = ocean_layer_depth.astype(jnp.float32)

    def one_block(block_index):
        indices = (block_index * block_rows - 2 + jnp.arange(block_rows + 4)).astype(jnp.int32)
        direct_ids = jnp.clip(indices, 0, entire_parallels - 1).astype(jnp.int32)
        mirror_ids = jnp.clip(2 * entire_parallels - 1 - indices, 0, entire_parallels - 1).astype(jnp.int32)

        def parallels_owned(source, factor):
            direct = jnp.take(source, direct_ids, axis=-2)
            mirror = jnp.flip(jnp.take(source, mirror_ids, axis=-2), -1) * factor
            picked = jnp.where((indices >= entire_parallels)[:, None], mirror, direct)
            picked = jnp.where((indices < 0)[:, None], jnp.zeros_like(picked), picked)
            return jnp.concatenate([picked[..., -2:], picked, picked[..., :2]], -1)

        joined_tracers = jnp.concatenate([parallels_owned(thermal_tracer, 1.0), parallels_owned(saltiness_tracer, 1.0),
                                   parallels_owned(eastward_transport, -1.0), parallels_owned(northward_transport, -1.0),
                                   parallels_owned(eastward_spacing, 1.0)[None], parallels_owned(southward_spacing, 1.0)[None],
                                   parallels_owned(bottom_float, 1.0)[None]], 0)
        return step_block(joined_tracers, layer_pile)

    new_temp, new_salt = lax.map(one_block, jnp.arange(N_LAT, dtype=jnp.int32))

    def joined(blocks):
        return jnp.moveaxis(blocks, 0, 1).reshape(layer_pile, entire_parallels, entire_meridians)

    return joined(new_temp), joined(new_salt)
```

```python
import jax
import jax.numpy as jnp
from jax import lax
from jax.experimental import pallas as pl
from jax.experimental.pallas import tpu as pltpu
from jax.sharding import PartitionSpec as P

MESH = pl.DeviceIdType.MESH
F32 = jnp.float32

TIME_STEP = 0.2
DIFFUSIVITY = 0.5
EXPANSION = 0.2
CONTRACTION = 0.8
STRAT_FLOOR = 0.5
SLOPE_LIMIT = 2.0

LEVELS = 6
ROWS = 32
LANES = 128


def turn(x, shift, axis):
    shift = shift % x.shape[axis]
    return x if shift == 0 else pltpu.roll(x, shift, axis)


def lane_reversed(x, lane):
    for bit in range(7):
        step = 1 << bit
        x = jnp.where((lane & step) == 0, turn(x, -step, 1), turn(x, step, 1))
    return x


def face_terms(speed, rlen):
    return speed >= 0.0, 0.5 - jnp.abs((0.5 * TIME_STEP) * speed * rlen)


def face_slope(rjump, rlen, strat):
    return jnp.clip(rjump * rlen / jnp.maximum(strat, STRAT_FLOOR), -SLOPE_LIMIT, SLOPE_LIMIT)


def face_flux(here, there, before, jump, after, gradient, slope, speed, upwind, factor, rlen):
    side = jnp.where(upwind, before, after)
    limited = jnp.maximum(jnp.minimum(side, jump), 0.0) + jnp.minimum(jnp.maximum(side, jump), 0.0)
    step = factor * limited
    value = jnp.where(upwind, here + step, there - step)
    return speed * value - DIFFUSIVITY * (jump * rlen - slope * gradient)


def vertical_quarter(sums):
    count = len(sums)
    return [0.25 * (sums[min(k + 1, count - 1)] - sums[max(k - 1, 0)]) for k in range(count)]


def kernel(
    temp_hbm, salt_hbm, east_hbm, north_hbm, dx_hbm, dy_hbm, depth_hbm,
    new_temp, new_salt,
    temp_in, salt_in, east_in, north_in, dx_in, dy_in, depth_in,
    held, result,
    pack_ts, pack_u, pack_g,
    own_rows, own_speed, own_geo,
    to_east, to_west, to_north, to_south,
    from_west, from_east, from_south, from_north,
    in_sem, out_sem, send_sem, recv_sem,
):
    lon, lat = lax.axis_index("lon"), lax.axis_index("lat")
    lon_count, lat_count = lax.axis_size("lon"), lax.axis_size("lat")
    west = (lax.rem(lon + lon_count - 1, lon_count), lat)
    east = (lax.rem(lon + 1, lon_count), lat)
    mirror = (lon_count - 1 - lon, lat)
    top = lat == lat_count - 1
    bottom = lat == 0

    barrier = pltpu.get_barrier_semaphore()

    def greet(device):
        pl.semaphore_signal(barrier, inc=1, device_id=device, device_id_type=MESH)

    greet(west)
    greet(east)

    @pl.when(top)
    def _():
        greet(mirror)

    @pl.when(jnp.logical_not(top))
    def _():
        greet((lon, lat + 1))

    @pl.when(jnp.logical_not(bottom))
    def _():
        greet((lon, lat - 1))

    pairs = [
        (depth_hbm, depth_in), (temp_hbm, temp_in), (salt_hbm, salt_in), (east_hbm, east_in),
        (dx_hbm, dx_in), (dy_hbm, dy_in), (north_hbm, north_in),
    ]
    loads = [pltpu.make_async_copy(a, b, in_sem.at[i]) for i, (a, b) in enumerate(pairs)]
    for load in loads:
        load.start()
    for load in loads:
        load.wait()

    lane8 = lax.broadcasted_iota(jnp.int32, (8, LANES), 1)
    sub8 = lax.broadcasted_iota(jnp.int32, (8, LANES), 0)
    slot = lane8 & 15
    group = lane8 >> 4

    depth = depth_in[...].astype(F32)
    for k in range(LEVELS):
        wet = depth > float(k)
        held[0, k] = jnp.where(wet, temp_in[k], 0.0)
        held[1, k] = jnp.where(wet, salt_in[k], 0.0)

    def gathered(blocks):
        total = turn(blocks[0], 4, 1)
        for g in range(1, len(blocks)):
            total = jnp.where(group == g, turn(blocks[g], 16 * g + 4, 1), total)
        return total

    def blocks_of(array):
        return [array[8 * r : 8 * r + 8] for r in range(ROWS // 8)]

    packed = []
    packed_u = []
    for k in range(LEVELS):
        packed.append(gathered(blocks_of(held[0, k]) + blocks_of(held[1, k])))
        packed_u.append(gathered(blocks_of(east_in[k]) * 2))
    dx, dy = dx_in[...], dy_in[...]
    packed_d = gathered(blocks_of(depth) * 2)
    packed_dx = gathered(blocks_of(dx) * 2)
    packed_dy = gathered(blocks_of(dy) * 2)

    eastward, westward, eastward_u = packed_d, packed_d, packed_d
    eastward, westward = turn(packed_d, 10, 1), turn(packed_d, 8, 1)
    eastward = jnp.where(slot == 14, turn(packed_dx, 11, 1), eastward)
    eastward = jnp.where(slot == 15, turn(packed_dy, 12, 1), eastward)
    westward = jnp.where(slot == 14, turn(packed_dx, 10, 1), westward)
    westward = jnp.where(slot == 15, turn(packed_dy, 11, 1), westward)
    eastward_u = turn(packed_u[0], -3, 1)
    for k in range(LEVELS):
        eastward = jnp.where((slot >> 1) == k, turn(packed[k], 2 * k - 2, 1), eastward)
        westward = jnp.where((slot >> 1) == k, turn(packed[k], 2 * k - 4, 1), westward)
        if k:
            eastward_u = jnp.where(slot == k, turn(packed_u[k], k - 3, 1), eastward_u)
    to_east[0:8] = eastward
    to_east[8:16] = eastward_u
    to_west[...] = westward

    for k in range(LEVELS):
        at = 8 * (k // 2) + 2 * (k % 2)
        for tracer in range(2):
            to_north[at + 4 * tracer : at + 4 * tracer + 2] = held[tracer, k, ROWS - 2 : ROWS]
            to_south[at + 4 * tracer : at + 4 * tracer + 2] = held[tracer, k, 0:2]
        to_north[28 + k : 29 + k] = north_in[k, ROWS - 1 : ROWS]
    to_north[24:26] = depth[ROWS - 2 : ROWS]
    to_north[26:27] = dx_in[ROWS - 1 : ROWS]
    to_north[27:28] = dy_in[ROWS - 1 : ROWS]
    to_north[34:40] = jnp.zeros((6, LANES), F32)
    to_south[24:26] = depth[0:2]
    to_south[26:27] = dx_in[0:1]
    to_south[27:28] = dy_in[0:1]
    to_south[28:32] = jnp.zeros((4, LANES), F32)

    @pl.when(top)
    def _():
        for block in range(4):
            x = to_north[8 * block : 8 * block + 8]
            swapped = jnp.where((sub8 & 1) == 0, turn(x, -1, 0), turn(x, 1, 0))
            if block == 3:
                swapped = jnp.where(sub8 < 2, swapped, x)
            to_north[8 * block : 8 * block + 8] = lane_reversed(swapped, lane8)

    @pl.when(bottom)
    def _():
        from_south[...] = jnp.zeros_like(from_south)

    pl.semaphore_wait(barrier, jnp.where(bottom, 3, 4))

    def remote(src, dst, index, device):
        return pltpu.make_async_remote_copy(
            src_ref=src, dst_ref=dst, send_sem=send_sem.at[index], recv_sem=recv_sem.at[index],
            device_id=device, device_id_type=MESH,
        )

    send_east = remote(to_east, from_west, 0, east)
    send_west = remote(to_west, from_east, 1, west)

    send_north = remote(to_north, from_south, 2, (lon, jnp.minimum(lat + 1, lat_count - 1)))
    send_south = remote(to_south, from_north, 3, (lon, jnp.maximum(lat - 1, 0)))
    send_east.start()
    send_west.start()

    @pl.when(top)
    def _():
        pltpu.make_async_remote_copy(
            src_ref=to_north.at[0:32], dst_ref=from_north, send_sem=send_sem.at[2], recv_sem=recv_sem.at[3],
            device_id=mirror, device_id_type=MESH,
        ).start()

    @pl.when(jnp.logical_not(top))
    def _():
        send_north.start()

    @pl.when(jnp.logical_not(bottom))
    def _():
        send_south.start()

    def opened(x):
        return jnp.where(slot < 4, x, turn(x, 4, 1))

    for k in range(LEVELS):
        pack_ts[k] = opened(packed[k])
        pack_u[k] = opened(packed_u[k])
    pack_g[0] = opened(packed_d)
    pack_g[1] = opened(packed_dx)
    pack_g[2] = opened(packed_dy)

    lane = lax.broadcasted_iota(jnp.int32, (ROWS, LANES), 1)
    row = lax.broadcasted_iota(jnp.int32, (ROWS, LANES), 0)
    inside_x = (lane >= 1) & (lane <= LANES - 3)
    inside_y = (row >= 1) & (row <= ROWS - 3)
    scale = -TIME_STEP / (dx * dy)

    def axis_part(axis, along, across, inside):
        size = LANES if axis else ROWS
        rlen = 2.0 / (along + turn(along, -1, axis))
        breadth = jnp.where(inside, 0.5 * (across + turn(across, -1, axis)), 0.0)
        least = jnp.minimum(depth, turn(depth, -1, axis))
        return rlen, breadth, least

    geo = [axis_part(1, dx, dy, inside_x), axis_part(0, dy, dx, inside_y)]

    def level_state(k):
        t, s = held[0, k], held[1, k]
        return [(t, s, turn(t, -1, a), turn(s, -1, a)) for a in (1, 0)]

    states = [level_state(k) for k in range(LEVELS)]
    for k in range(LEVELS):
        divergence = [0.0, 0.0]
        for position, axis in enumerate((1, 0)):
            rlen, breadth, least = geo[position]
            t, s, t1, s1 = states[k][position]
            up, down = states[min(k + 1, LEVELS - 1)][position], states[max(k - 1, 0)][position]
            gt = 0.25 * ((up[0] + up[2]) - (down[0] + down[2]))
            gs = 0.25 * ((up[1] + up[3]) - (down[1] + down[3]))
            face = least > float(k)
            jt = jnp.where(face, t1 - t, 0.0)
            js = jnp.where(face, s1 - s, 0.0)
            speed = (east_in if axis else north_in)[k]
            upwind, factor = face_terms(speed, rlen)
            slope = face_slope(CONTRACTION * js - EXPANSION * jt, rlen, CONTRACTION * gs - EXPANSION * gt)
            weight = jnp.where(face, breadth, 0.0)
            for tracer, (a, b, j, g) in enumerate(((t, t1, jt, gt), (s, s1, js, gs))):
                flux = weight * face_flux(
                    a, b, turn(j, 1, axis), j, turn(j, -1, axis), g, slope, speed, upwind, factor, rlen
                )
                divergence[tracer] = divergence[tracer] + (flux - turn(flux, 1, axis))
        wet = depth > float(k)
        for tracer in range(2):
            result[tracer, k] = held[tracer, k] + jnp.where(wet, scale * divergence[tracer], 0.0)

    odd = sub8 & 3
    own_mix = jnp.where(sub8 < 4, -EXPANSION, CONTRACTION)
    other_mix = jnp.where(sub8 < 4, CONTRACTION, -EXPANSION)
    lane_mix = jnp.where(lane8 < 64, -EXPANSION, CONTRACTION)
    lane_other = jnp.where(lane8 < 64, CONTRACTION, -EXPANSION)

    spans = ((2, 4, 29, 31), (1, 2, 0, 1), (2, 4, 30, 32), (0, 2, 0, 2), (2, 3, 31, 32), (0, 2, 1, 3))
    places = (0, 1, 1, 2, 2, 3)
    for place, (lo, hi, first, last) in zip(places, spans):
        for tracer in range(2):
            at = 4 * tracer
            for k in range(LEVELS):
                own_rows[place, k, at + lo : at + hi] = held[tracer, k, first:last]
            own_geo[place, at + lo : at + hi] = depth[first:last]
    for tracer in range(2):
        at = 4 * tracer
        for k in range(LEVELS):
            own_speed[k, at + 1 : at + 2] = north_in[k, 0:1]
            own_speed[k, at + 2 : at + 4] = north_in[k, 30:32]
        for which, source in ((4, dx_in), (6, dy_in)):
            own_geo[which, at + 1 : at + 2] = source[0:1]
            own_geo[which, at + 2 : at + 4] = source[30:32]
            own_geo[which + 1, at : at + 2] = source[0:2]
            own_geo[which + 1, at + 2 : at + 3] = source[31:32]
        own_geo[8, at : at + 2] = scale[0:2]
        own_geo[8, at + 2 : at + 4] = scale[30:32]
        own_geo[9, at : at + 2] = depth[0:2]
        own_geo[9, at + 2 : at + 4] = depth[30:32]

    @pl.when(jnp.logical_not(bottom))
    def _():
        remote(to_north, from_south, 2, (lon, lat)).wait_recv()

    remote(to_south, from_north, 3, (lon, lat)).wait_recv()

    def spread(ref, index):
        return jnp.broadcast_to(ref[index : index + 1], (8, LANES))

    depth_a = jnp.where(odd == 0, spread(from_south, 24), jnp.where(odd == 1, spread(from_south, 25), own_geo[0]))
    depth_b = jnp.where(odd == 0, spread(from_south, 25), own_geo[1])
    depth_c = jnp.where(odd == 3, spread(from_north, 24), own_geo[2])
    depth_d = jnp.where(odd == 2, spread(from_north, 24), jnp.where(odd == 3, spread(from_north, 25), own_geo[3]))
    dx_b = jnp.where(odd == 0, spread(from_south, 26), own_geo[4])
    dx_c = jnp.where(odd == 3, spread(from_north, 26), own_geo[5])
    dy_b = jnp.where(odd == 0, spread(from_south, 27), own_geo[6])
    dy_c = jnp.where(odd == 3, spread(from_north, 27), own_geo[7])
    rlen = 2.0 / (dy_b + dy_c)
    breadth = 0.5 * (dx_b + dx_c)
    least_w, least_m, least_e = (
        jnp.minimum(depth_a, depth_b), jnp.minimum(depth_b, depth_c), jnp.minimum(depth_c, depth_d)
    )
    operands = []
    for k in range(LEVELS):
        south = from_south[8 * (k // 2) : 8 * (k // 2) + 8]
        north = from_north[8 * (k // 2) : 8 * (k // 2) + 8]
        south = turn(south, -2 * (k % 2), 0)
        north = turn(north, 2 - 2 * (k % 2), 0)
        operands.append((
            jnp.where(odd < 2, south, own_rows[0, k]),
            jnp.where(odd == 0, turn(south, -1, 0), own_rows[1, k]),
            jnp.where(odd == 3, turn(north, 1, 0), own_rows[2, k]),
            jnp.where(odd >= 2, north, own_rows[3, k]),
        ))
    gradients = vertical_quarter([b + c for _, b, c, _ in operands])
    for k in range(LEVELS):
        a, b, c, d = operands[k]
        jump = jnp.where(least_m > float(k), c - b, 0.0)
        before = jnp.where(least_w > float(k), b - a, 0.0)
        after = jnp.where(least_e > float(k), d - c, 0.0)
        gradient = gradients[k]
        speed = jnp.where(odd == 0, spread(from_south, 28 + k), own_speed[k])
        upwind, factor = face_terms(speed, rlen)
        slope = face_slope(
            own_mix * jump + other_mix * turn(jump, 4, 0), rlen, own_mix * gradient + other_mix * turn(gradient, 4, 0)
        )
        flux = jnp.where(least_m > float(k), breadth, 0.0) * face_flux(
            b, c, before, jump, after, gradient, slope, speed, upwind, factor, rlen
        )
        change = jnp.where(
            odd == 0, turn(flux, -1, 0) - flux,
            jnp.where(odd == 1, -flux, jnp.where(odd == 2, flux, flux - turn(flux, 1, 0))),
        )
        change = jnp.where(own_geo[9] > float(k), own_geo[8] * change, 0.0)
        for tracer in range(2):
            at = 4 * tracer
            result[tracer, k, 0:2] += change[at : at + 2]
            result[tracer, k, ROWS - 2 : ROWS] += change[at + 2 : at + 4]

    remote(to_east, from_west, 0, (lon, lat)).wait_recv()
    remote(to_west, from_east, 1, (lon, lat)).wait_recv()
    came_w, came_u, came_e = from_west[0:8], from_west[8:16], from_east[...]

    def closed(own, low, high, low_from, high_from):
        x = jnp.where((slot >> 1) == 3, turn(low, 6 - low_from, 1), own)
        return jnp.where((slot >> 1) == 2, turn(high, 4 - high_from, 1), x)

    depth_x = closed(pack_g[0], came_w, came_e, 12, 12)
    own_dx, own_dy = pack_g[1], pack_g[2]
    dx_x = closed(own_dx, came_w, came_e, 13, 14)
    dy_x = closed(own_dy, came_w, came_e, 14, 15)
    rlen = 2.0 / (dx_x + turn(dx_x, -1, 1))
    breadth = 0.5 * (dy_x + turn(dy_x, -1, 1))
    edge = (slot == 2) | (slot == 3) | (slot == 7) | (slot == 8)
    breadth = jnp.where(edge, breadth, 0.0)
    least = jnp.minimum(depth_x, turn(depth_x, -1, 1))
    weight_x = -TIME_STEP / (dx_x * dy_x)
    values = [closed(pack_ts[k], came_w, came_e, 2 * k, 2 * k) for k in range(LEVELS)]
    nexts = [turn(x, -1, 1) for x in values]
    gradients = vertical_quarter([x + y for x, y in zip(values, nexts)])
    for k in range(LEVELS):
        face = least > float(k)
        jump = jnp.where(face, nexts[k] - values[k], 0.0)
        gradient = gradients[k]
        speed = jnp.where(slot == 7, turn(came_u, 7 - k, 1), pack_u[k])
        upwind, factor = face_terms(speed, rlen)
        slope = face_slope(
            lane_mix * jump + lane_other * turn(jump, 64, 1), rlen,
            lane_mix * gradient + lane_other * turn(gradient, 64, 1),
        )
        flux = jnp.where(face, breadth, 0.0) * face_flux(
            values[k], nexts[k], turn(jump, 1, 1), jump, turn(jump, -1, 1), gradient, slope, speed, upwind, factor,
            rlen,
        )
        change = flux - turn(flux, 1, 1)
        change = jnp.where(depth_x > float(k), weight_x * change, 0.0)
        change = jnp.where(slot < 4, change, turn(change, -4, 1))
        for tracer in range(2):
            for r in range(ROWS // 8):
                moved = turn(change, 124 - 64 * tracer - 16 * r, 1)
                result[tracer, k, 8 * r : 8 * r + 8] += jnp.where((lane8 < 2) | (lane8 >= 126), moved, 0.0)

    stores = [
        pltpu.make_async_copy(result.at[0], new_temp, out_sem.at[0]),
        pltpu.make_async_copy(result.at[1], new_salt, out_sem.at[1]),
    ]
    for store in stores:
        store.start()
    send_east.wait_send()
    send_west.wait_send()

    @pl.when(top)
    def _():
        pltpu.make_async_remote_copy(
            src_ref=to_north.at[0:32], dst_ref=from_north, send_sem=send_sem.at[2], recv_sem=recv_sem.at[3],
            device_id=mirror, device_id_type=MESH,
        ).wait_send()

    @pl.when(jnp.logical_not(top))
    def _():
        send_north.wait_send()

    @pl.when(jnp.logical_not(bottom))
    def _():
        send_south.wait_send()

    for store in stores:
        store.wait()


def local(temp, salt, east, north, dx, dy, depth):
    full = (LEVELS, ROWS, LANES)
    flat = (ROWS, LANES)
    shape = jax.ShapeDtypeStruct(full, F32)
    scratch = [
        pltpu.VMEM(full, F32), pltpu.VMEM(full, F32), pltpu.VMEM(full, F32), pltpu.VMEM(full, F32),
        pltpu.VMEM(flat, F32), pltpu.VMEM(flat, F32), pltpu.VMEM(flat, jnp.int32),
        pltpu.VMEM((2,) + full, F32), pltpu.VMEM((2,) + full, F32),
        pltpu.VMEM((LEVELS, 8, LANES), F32), pltpu.VMEM((LEVELS, 8, LANES), F32), pltpu.VMEM((3, 8, LANES), F32),
        pltpu.VMEM((4, LEVELS, 8, LANES), F32), pltpu.VMEM((LEVELS, 8, LANES), F32), pltpu.VMEM((10, 8, LANES), F32),
        pltpu.VMEM((16, LANES), F32), pltpu.VMEM((8, LANES), F32), pltpu.VMEM((40, LANES), F32), pltpu.VMEM((32, LANES), F32),
        pltpu.VMEM((16, LANES), F32), pltpu.VMEM((8, LANES), F32), pltpu.VMEM((40, LANES), F32), pltpu.VMEM((32, LANES), F32),
        pltpu.SemaphoreType.DMA((7,)), pltpu.SemaphoreType.DMA((2,)),
        pltpu.SemaphoreType.DMA((4,)), pltpu.SemaphoreType.DMA((4,)),
    ]
    return pl.pallas_call(
        kernel,
        out_shape=(shape, shape),
        in_specs=[pl.BlockSpec(memory_space=pl.ANY)] * 7,
        out_specs=(pl.BlockSpec(memory_space=pl.ANY),) * 2,
        scratch_shapes=scratch,
        compiler_params=pltpu.CompilerParams(collective_id=0, has_side_effects=True),
        name="tracer_step",
    )(temp, salt, east, north, dx, dy, depth)


def solution(mesh):
    full = P(None, "lat", "lon")
    flat = P("lat", "lon")
    return jax.shard_map(
        local, mesh=mesh, in_specs=(full,) * 4 + (flat,) * 3, out_specs=(full, full), check_vma=False
    )
```

```python
import jax
import jax.numpy as jnp
from jax import lax
from jax.experimental import pallas as pl
from jax.experimental.pallas import tpu as pltpu
from jax.sharding import PartitionSpec as P

MESH = pl.DeviceIdType.MESH
F32 = jnp.float32

TIME_STEP = 0.2
DIFFUSIVITY = 0.5
EXPANSION = 0.2
CONTRACTION = 0.8
STRAT_FLOOR = 0.5
SLOPE_LIMIT = 2.0

LEVELS = 6
ROWS = 32
LANES = 128


def turn(x, shift, axis):
    shift = shift % x.shape[axis]
    return x if shift == 0 else pltpu.roll(x, shift, axis)


def lane_reversed(x, lane):
    for bit in range(7):
        step = 1 << bit
        x = jnp.where((lane & step) == 0, turn(x, -step, 1), turn(x, step, 1))
    return x


def face_terms(speed, rlen):
    return speed >= 0.0, 0.5 - jnp.abs((0.5 * TIME_STEP) * speed * rlen)


def face_slope(rjump, rlen, strat):
    return jnp.clip(rjump * rlen / jnp.maximum(strat, STRAT_FLOOR), -SLOPE_LIMIT, SLOPE_LIMIT)


def face_flux(here, there, before, jump, after, gradient, slope, speed, upwind, factor, rlen):
    side = jnp.where(upwind, before, after)
    limited = jnp.maximum(jnp.minimum(side, jump), 0.0) + jnp.minimum(jnp.maximum(side, jump), 0.0)
    step = factor * limited
    value = jnp.where(upwind, here + step, there - step)
    return speed * value - DIFFUSIVITY * (jump * rlen - slope * gradient)


def vertical_quarter(sums):
    count = len(sums)
    return [0.25 * (sums[min(k + 1, count - 1)] - sums[max(k - 1, 0)]) for k in range(count)]


def kernel(
    temp_hbm, salt_hbm, east_hbm, north_hbm, dx_hbm, dy_hbm, depth_hbm,
    result, changes,
    temp_in, salt_in, east_in, north_in, dx_in, dy_in, depth_in,
    held,
    pack_ts, pack_u, pack_g,
    own_rows, own_speed, own_geo,
    to_east, to_west, to_north, to_south,
    from_west, from_east, from_south, from_north,
    in_sem, send_sem, recv_sem,
):
    lon, lat = lax.axis_index("lon"), lax.axis_index("lat")
    lon_count, lat_count = lax.axis_size("lon"), lax.axis_size("lat")
    west = (lax.rem(lon + lon_count - 1, lon_count), lat)
    east = (lax.rem(lon + 1, lon_count), lat)
    mirror = (lon_count - 1 - lon, lat)
    north = (lon, jnp.minimum(lat + 1, lat_count - 1))
    south = (lon, jnp.maximum(lat - 1, 0))
    top = lat == lat_count - 1
    bottom = lat == 0

    place = lax.rem(lon, 4)
    even = lax.rem(lat, 2) == 0
    leads_east = place >= 2
    leads_west = (place == 1) | (place == 2)
    leads_mirror = place >= 2
    leads_north = even | (top & leads_mirror)
    leads_south = even & jnp.logical_not(bottom)
    answers_east = place <= 1
    answers_west = (place == 0) | (place == 3)
    answers_south = jnp.logical_not(even)

    pairs = [
        (depth_hbm, depth_in), (temp_hbm, temp_in), (salt_hbm, salt_in), (east_hbm, east_in),
        (dx_hbm, dx_in), (dy_hbm, dy_in), (north_hbm, north_in),
    ]
    loads = [pltpu.make_async_copy(a, b, in_sem.at[i]) for i, (a, b) in enumerate(pairs)]
    for load in loads:
        load.start()

    barrier = pltpu.get_barrier_semaphore()

    def greet(device):
        pl.semaphore_signal(barrier, inc=1, device_id=device, device_id_type=MESH)

    @pl.when(answers_east)
    def _():
        greet(east)

    @pl.when(answers_west)
    def _():
        greet(west)

    @pl.when(jnp.logical_not(even))
    def _():
        greet(south)

    @pl.when(jnp.logical_not(even | top))
    def _():
        greet(north)

    @pl.when(top & jnp.logical_not(leads_mirror))
    def _():
        greet(mirror)

    def one(flag):
        return jnp.where(flag, 1, 0)

    announced = (
        one(leads_east) + one(leads_west) + one(even) + one(leads_south) + one(top & leads_mirror)
    )

    def remote(src, dst, out, into, device):
        return pltpu.make_async_remote_copy(
            src_ref=src, dst_ref=dst, send_sem=send_sem.at[out], recv_sem=recv_sem.at[into],
            device_id=device, device_id_type=MESH,
        )

    def send_east():
        return remote(to_east, from_west, 0, 0, east)

    def send_west():
        return remote(to_west, from_east, 1, 1, west)

    def send_north():
        return remote(to_north, from_south, 2, 2, north)

    def send_mirror():
        return remote(to_north.at[0:32], from_north, 2, 3, mirror)

    def send_south():
        return remote(to_south, from_north, 3, 3, south)

    def start_northward():
        @pl.when(top)
        def _():
            send_mirror().start()

        @pl.when(jnp.logical_not(top))
        def _():
            send_north().start()

    for load in loads[:3]:
        load.wait()

    lane8 = lax.broadcasted_iota(jnp.int32, (8, LANES), 1)
    sub8 = lax.broadcasted_iota(jnp.int32, (8, LANES), 0)
    slot = lane8 & 15
    group = lane8 >> 4

    depth = depth_in[...].astype(F32)
    for k in range(LEVELS):
        wet = depth > float(k)
        held[0, k] = jnp.where(wet, temp_in[k], 0.0)
        held[1, k] = jnp.where(wet, salt_in[k], 0.0)

    def gathered(blocks):
        total = turn(blocks[0], 4, 1)
        for g in range(1, len(blocks)):
            total = jnp.where(group == g, turn(blocks[g], 16 * g + 4, 1), total)
        return total

    def blocks_of(array):
        return [array[8 * r : 8 * r + 8] for r in range(ROWS // 8)]

    packed = []
    packed_u = []
    for k in range(LEVELS):
        packed.append(gathered(blocks_of(held[0, k]) + blocks_of(held[1, k])))
    for load in loads[3:6]:
        load.wait()
    for k in range(LEVELS):
        packed_u.append(gathered(blocks_of(east_in[k]) * 2))
    dx, dy = dx_in[...], dy_in[...]
    packed_d = gathered(blocks_of(depth) * 2)
    packed_dx = gathered(blocks_of(dx) * 2)
    packed_dy = gathered(blocks_of(dy) * 2)

    eastward, westward = turn(packed_d, 10, 1), turn(packed_d, 8, 1)
    eastward = jnp.where(slot == 14, turn(packed_dx, 11, 1), eastward)
    eastward = jnp.where(slot == 15, turn(packed_dy, 12, 1), eastward)
    westward = jnp.where(slot == 14, turn(packed_dx, 10, 1), westward)
    westward = jnp.where(slot == 15, turn(packed_dy, 11, 1), westward)
    eastward_u = turn(packed_u[0], -3, 1)
    for k in range(LEVELS):
        eastward = jnp.where((slot >> 1) == k, turn(packed[k], 2 * k - 2, 1), eastward)
        westward = jnp.where((slot >> 1) == k, turn(packed[k], 2 * k - 4, 1), westward)
        if k:
            eastward_u = jnp.where(slot == k, turn(packed_u[k], k - 3, 1), eastward_u)
    to_east[0:8] = eastward
    to_east[8:16] = eastward_u
    to_west[...] = westward

    @pl.when(announced > 0)
    def _():
        pl.semaphore_wait(barrier, announced)

    @pl.when(leads_east)
    def _():
        send_east().start()

    @pl.when(leads_west)
    def _():
        send_west().start()

    loads[6].wait()

    for k in range(LEVELS):
        at = 8 * (k // 2) + 2 * (k % 2)
        for tracer in range(2):
            to_north[at + 4 * tracer : at + 4 * tracer + 2] = held[tracer, k, ROWS - 2 : ROWS]
            to_south[at + 4 * tracer : at + 4 * tracer + 2] = held[tracer, k, 0:2]
        to_north[28 + k : 29 + k] = north_in[k, ROWS - 1 : ROWS]
    to_north[24:26] = depth[ROWS - 2 : ROWS]
    to_north[26:27] = dx_in[ROWS - 1 : ROWS]
    to_north[27:28] = dy_in[ROWS - 1 : ROWS]
    to_north[34:40] = jnp.zeros((6, LANES), F32)
    to_south[24:26] = depth[0:2]
    to_south[26:27] = dx_in[0:1]
    to_south[27:28] = dy_in[0:1]
    to_south[28:32] = jnp.zeros((4, LANES), F32)

    @pl.when(top)
    def _():
        for block in range(4):
            x = to_north[8 * block : 8 * block + 8]
            swapped = jnp.where((sub8 & 1) == 0, turn(x, -1, 0), turn(x, 1, 0))
            if block == 3:
                swapped = jnp.where(sub8 < 2, swapped, x)
            to_north[8 * block : 8 * block + 8] = lane_reversed(swapped, lane8)

    @pl.when(bottom)
    def _():
        from_south[...] = jnp.zeros_like(from_south)

    @pl.when(leads_north)
    def _():
        start_northward()

    @pl.when(leads_south)
    def _():
        send_south().start()

    def opened(x):
        return jnp.where(slot < 4, x, turn(x, 4, 1))

    for k in range(LEVELS):
        pack_ts[k] = opened(packed[k])
        pack_u[k] = opened(packed_u[k])
    pack_g[0] = opened(packed_d)
    pack_g[1] = opened(packed_dx)
    pack_g[2] = opened(packed_dy)

    lane = lax.broadcasted_iota(jnp.int32, (ROWS, LANES), 1)
    row = lax.broadcasted_iota(jnp.int32, (ROWS, LANES), 0)
    inside_x = (lane >= 1) & (lane <= LANES - 3)
    inside_y = (row >= 1) & (row <= ROWS - 3)
    scale = -TIME_STEP / (dx * dy)

    def axis_part(axis, along, across, inside):
        size = LANES if axis else ROWS
        rlen = 2.0 / (along + turn(along, -1, axis))
        breadth = jnp.where(inside, 0.5 * (across + turn(across, -1, axis)), 0.0)
        least = jnp.minimum(depth, turn(depth, -1, axis))
        return rlen, breadth, least

    geo = [axis_part(1, dx, dy, inside_x), axis_part(0, dy, dx, inside_y)]

    def level_state(k):
        t, s = held[0, k], held[1, k]
        return [(t, s, turn(t, -1, a), turn(s, -1, a)) for a in (1, 0)]

    states = [level_state(k) for k in range(LEVELS)]
    for k in range(LEVELS):
        divergence = [0.0, 0.0]
        for position, axis in enumerate((1, 0)):
            rlen, breadth, least = geo[position]
            t, s, t1, s1 = states[k][position]
            up, down = states[min(k + 1, LEVELS - 1)][position], states[max(k - 1, 0)][position]
            gt = 0.25 * ((up[0] + up[2]) - (down[0] + down[2]))
            gs = 0.25 * ((up[1] + up[3]) - (down[1] + down[3]))
            face = least > float(k)
            jt = jnp.where(face, t1 - t, 0.0)
            js = jnp.where(face, s1 - s, 0.0)
            speed = (east_in if axis else north_in)[k]
            upwind, factor = face_terms(speed, rlen)
            slope = face_slope(CONTRACTION * js - EXPANSION * jt, rlen, CONTRACTION * gs - EXPANSION * gt)
            weight = jnp.where(face, breadth, 0.0)
            for tracer, (a, b, j, g) in enumerate(((t, t1, jt, gt), (s, s1, js, gs))):
                flux = weight * face_flux(
                    a, b, turn(j, 1, axis), j, turn(j, -1, axis), g, slope, speed, upwind, factor, rlen
                )
                divergence[tracer] = divergence[tracer] + (flux - turn(flux, 1, axis))
        wet = depth > float(k)
        for tracer in range(2):
            result[tracer, k] = held[tracer, k] + jnp.where(wet, scale * divergence[tracer], 0.0)

    odd = sub8 & 3
    own_mix = jnp.where(sub8 < 4, -EXPANSION, CONTRACTION)
    other_mix = jnp.where(sub8 < 4, CONTRACTION, -EXPANSION)
    lane_mix = jnp.where(lane8 < 64, -EXPANSION, CONTRACTION)
    lane_other = jnp.where(lane8 < 64, CONTRACTION, -EXPANSION)

    spans = ((2, 4, 29, 31), (1, 2, 0, 1), (2, 4, 30, 32), (0, 2, 0, 2), (2, 3, 31, 32), (0, 2, 1, 3))
    operand_ids = (0, 1, 1, 2, 2, 3)
    for which, (lo, hi, first, last) in zip(operand_ids, spans):
        for tracer in range(2):
            at = 4 * tracer
            for k in range(LEVELS):
                own_rows[which, k, at + lo : at + hi] = held[tracer, k, first:last]
            own_geo[which, at + lo : at + hi] = depth[first:last]
    for tracer in range(2):
        at = 4 * tracer
        for k in range(LEVELS):
            own_speed[k, at + 1 : at + 2] = north_in[k, 0:1]
            own_speed[k, at + 2 : at + 4] = north_in[k, 30:32]
        for which, source in ((4, dx_in), (6, dy_in)):
            own_geo[which, at + 1 : at + 2] = source[0:1]
            own_geo[which, at + 2 : at + 4] = source[30:32]
            own_geo[which + 1, at : at + 2] = source[0:2]
            own_geo[which + 1, at + 2 : at + 3] = source[31:32]
        own_geo[8, at : at + 2] = scale[0:2]
        own_geo[8, at + 2 : at + 4] = scale[30:32]
        own_geo[9, at : at + 2] = depth[0:2]
        own_geo[9, at + 2 : at + 4] = depth[30:32]

    @pl.when(jnp.logical_not(bottom))
    def _():
        send_north().wait_recv()

    @pl.when(answers_south)
    def _():
        send_south().start()

    send_south().wait_recv()

    @pl.when(jnp.logical_not(leads_north))
    def _():
        start_northward()

    def spread(ref, index):
        return jnp.broadcast_to(ref[index : index + 1], (8, LANES))

    depth_a = jnp.where(odd == 0, spread(from_south, 24), jnp.where(odd == 1, spread(from_south, 25), own_geo[0]))
    depth_b = jnp.where(odd == 0, spread(from_south, 25), own_geo[1])
    depth_c = jnp.where(odd == 3, spread(from_north, 24), own_geo[2])
    depth_d = jnp.where(odd == 2, spread(from_north, 24), jnp.where(odd == 3, spread(from_north, 25), own_geo[3]))
    dx_b = jnp.where(odd == 0, spread(from_south, 26), own_geo[4])
    dx_c = jnp.where(odd == 3, spread(from_north, 26), own_geo[5])
    dy_b = jnp.where(odd == 0, spread(from_south, 27), own_geo[6])
    dy_c = jnp.where(odd == 3, spread(from_north, 27), own_geo[7])
    rlen = 2.0 / (dy_b + dy_c)
    breadth = 0.5 * (dx_b + dx_c)
    least_w, least_m, least_e = (
        jnp.minimum(depth_a, depth_b), jnp.minimum(depth_b, depth_c), jnp.minimum(depth_c, depth_d)
    )
    operands = []
    for k in range(LEVELS):
        south = from_south[8 * (k // 2) : 8 * (k // 2) + 8]
        north = from_north[8 * (k // 2) : 8 * (k // 2) + 8]
        south = turn(south, -2 * (k % 2), 0)
        north = turn(north, 2 - 2 * (k % 2), 0)
        operands.append((
            jnp.where(odd < 2, south, own_rows[0, k]),
            jnp.where(odd == 0, turn(south, -1, 0), own_rows[1, k]),
            jnp.where(odd == 3, turn(north, 1, 0), own_rows[2, k]),
            jnp.where(odd >= 2, north, own_rows[3, k]),
        ))
    gradients = vertical_quarter([b + c for _, b, c, _ in operands])
    for k in range(LEVELS):
        a, b, c, d = operands[k]
        jump = jnp.where(least_m > float(k), c - b, 0.0)
        before = jnp.where(least_w > float(k), b - a, 0.0)
        after = jnp.where(least_e > float(k), d - c, 0.0)
        gradient = gradients[k]
        speed = jnp.where(odd == 0, spread(from_south, 28 + k), own_speed[k])
        upwind, factor = face_terms(speed, rlen)
        slope = face_slope(
            own_mix * jump + other_mix * turn(jump, 4, 0), rlen, own_mix * gradient + other_mix * turn(gradient, 4, 0)
        )
        flux = jnp.where(least_m > float(k), breadth, 0.0) * face_flux(
            b, c, before, jump, after, gradient, slope, speed, upwind, factor, rlen
        )
        change = jnp.where(
            odd == 0, turn(flux, -1, 0) - flux,
            jnp.where(odd == 1, -flux, jnp.where(odd == 2, flux, flux - turn(flux, 1, 0))),
        )
        change = jnp.where(own_geo[9] > float(k), own_geo[8] * change, 0.0)
        for tracer in range(2):
            at = 4 * tracer
            result[tracer, k, 0:2] += change[at : at + 2]
            result[tracer, k, ROWS - 2 : ROWS] += change[at + 2 : at + 4]

    west_first = place == 3

    @pl.when(west_first)
    def _():
        send_east().wait_recv()
        send_west().start()

    send_west().wait_recv()

    @pl.when(answers_east)
    def _():
        send_east().start()

    @pl.when(jnp.logical_not(west_first))
    def _():
        send_east().wait_recv()

    @pl.when(place == 0)
    def _():
        send_west().start()

    came_w, came_u, came_e = from_west[0:8], from_west[8:16], from_east[...]

    def closed(own, low, high, low_from, high_from):
        x = jnp.where((slot >> 1) == 3, turn(low, 6 - low_from, 1), own)
        return jnp.where((slot >> 1) == 2, turn(high, 4 - high_from, 1), x)

    depth_x = closed(pack_g[0], came_w, came_e, 12, 12)
    own_dx, own_dy = pack_g[1], pack_g[2]
    dx_x = closed(own_dx, came_w, came_e, 13, 14)
    dy_x = closed(own_dy, came_w, came_e, 14, 15)
    rlen = 2.0 / (dx_x + turn(dx_x, -1, 1))
    breadth = 0.5 * (dy_x + turn(dy_x, -1, 1))
    edge = (slot == 2) | (slot == 3) | (slot == 7) | (slot == 8)
    breadth = jnp.where(edge, breadth, 0.0)
    least = jnp.minimum(depth_x, turn(depth_x, -1, 1))
    weight_x = -TIME_STEP / (dx_x * dy_x)
    values = [closed(pack_ts[k], came_w, came_e, 2 * k, 2 * k) for k in range(LEVELS)]
    nexts = [turn(x, -1, 1) for x in values]
    gradients = vertical_quarter([x + y for x, y in zip(values, nexts)])
    for k in range(LEVELS):
        face = least > float(k)
        jump = jnp.where(face, nexts[k] - values[k], 0.0)
        gradient = gradients[k]
        speed = jnp.where(slot == 7, turn(came_u, 7 - k, 1), pack_u[k])
        upwind, factor = face_terms(speed, rlen)
        slope = face_slope(
            lane_mix * jump + lane_other * turn(jump, 64, 1), rlen,
            lane_mix * gradient + lane_other * turn(gradient, 64, 1),
        )
        flux = jnp.where(face, breadth, 0.0) * face_flux(
            values[k], nexts[k], turn(jump, 1, 1), jump, turn(jump, -1, 1), gradient, slope, speed, upwind, factor,
            rlen,
        )
        change = flux - turn(flux, 1, 1)
        change = jnp.where(depth_x > float(k), weight_x * change, 0.0)
        change = jnp.where(slot < 4, change, turn(change, -4, 1))
        changes[k] = change

    send_east().wait_send()
    send_west().wait_send()

    @pl.when(top)
    def _():
        send_mirror().wait_send()

    @pl.when(jnp.logical_not(top))
    def _():
        send_north().wait_send()

    @pl.when(jnp.logical_not(bottom))
    def _():
        send_south().wait_send()


def finish(result, changes, new_temp, new_salt):
    lane = lax.broadcasted_iota(jnp.int32, (8, LANES), 1)
    edge = (lane < 2) | (lane >= LANES - 2)
    for k in range(LEVELS):
        change = changes[k]
        for tracer, new in enumerate((new_temp, new_salt)):
            for r in range(ROWS // 8):
                moved = turn(change, 124 - 64 * tracer - 16 * r, 1)
                rows = slice(8 * r, 8 * r + 8)
                new[k, rows] = result[tracer, k, rows] + jnp.where(edge, moved, 0.0)


def local(temp, salt, east, north, dx, dy, depth):
    full = (LEVELS, ROWS, LANES)
    flat = (ROWS, LANES)
    shape = jax.ShapeDtypeStruct(full, F32)
    parts = ((2,) + full, (LEVELS, 8, LANES))
    message = [pltpu.VMEM((rows, LANES), F32) for rows in (16, 8, 40, 32)]
    scratch = [pltpu.VMEM(full, F32)] * 4 + [
        pltpu.VMEM(flat, F32), pltpu.VMEM(flat, F32), pltpu.VMEM(flat, jnp.int32),
        pltpu.VMEM((2,) + full, F32),
        pltpu.VMEM((LEVELS, 8, LANES), F32), pltpu.VMEM((LEVELS, 8, LANES), F32), pltpu.VMEM((3, 8, LANES), F32),
        pltpu.VMEM((4, LEVELS, 8, LANES), F32), pltpu.VMEM((LEVELS, 8, LANES), F32), pltpu.VMEM((10, 8, LANES), F32),
        *message, *message,
        pltpu.SemaphoreType.DMA((7,)), pltpu.SemaphoreType.DMA((4,)), pltpu.SemaphoreType.DMA((4,)),
    ]
    inner = pl.BlockSpec(memory_space=pltpu.VMEM)
    result, changes = pl.pallas_call(
        kernel,
        out_shape=tuple(pltpu.VMEM(part, F32) for part in parts),
        in_specs=[pl.BlockSpec(memory_space=pltpu.HBM)] * 7,
        out_specs=(inner, inner),
        scratch_shapes=scratch,
        compiler_params=pltpu.CompilerParams(
            collective_id=0, has_side_effects=True, vmem_limit_bytes=16 * 2**20
        ),
        name="tracer_step",
    )(*(pltpu.with_memory_space_constraint(x, pltpu.HBM) for x in (temp, salt, east, north, dx, dy, depth)))
    return pl.pallas_call(
        finish,
        out_shape=(shape, shape),
        in_specs=[inner, inner],
        out_specs=(inner, inner),
        compiler_params=pltpu.CompilerParams(vmem_limit_bytes=16 * 2**20),
        name="edge_columns",
    )(*(pltpu.with_memory_space_constraint(x, pltpu.VMEM) for x in (result, changes)))


def solution(mesh):
    full = P(None, "lat", "lon")
    flat = P("lat", "lon")
    return jax.shard_map(
        local, mesh=mesh, in_specs=(full,) * 4 + (flat,) * 3, out_specs=(full, full), check_vma=False
    )
```

```python
import jax
import jax.numpy as jnp
from jax import lax
from jax.experimental import pallas as pl
from jax.experimental.pallas import tpu as pltpu
from jax.sharding import PartitionSpec as P

MESH = pl.DeviceIdType.MESH
F32 = jnp.float32

TIME_STEP = 0.2
DIFFUSIVITY = 0.5
EXPANSION = 0.2
CONTRACTION = 0.8
STRAT_FLOOR = 0.5
SLOPE_LIMIT = 2.0

LEVELS = 6
ROWS = 32
LANES = 128
PIECE = 3


def turn(x, shift, axis):
    shift = shift % x.shape[axis]
    return x if shift == 0 else pltpu.roll(x, shift, axis)


def lane_reversed(x, lane):
    for bit in range(7):
        step = 1 << bit
        x = jnp.where((lane & step) == 0, turn(x, -step, 1), turn(x, step, 1))
    return x


def face_terms(speed, rlen):
    return speed >= 0.0, 0.5 - jnp.abs((0.5 * TIME_STEP) * speed * rlen)


def face_slope(rjump, rlen, strat):
    return jnp.clip(rjump * rlen / jnp.maximum(strat, STRAT_FLOOR), -SLOPE_LIMIT, SLOPE_LIMIT)


def face_flux(here, there, before, jump, after, gradient, slope, speed, upwind, factor, rlen):
    side = jnp.where(upwind, before, after)
    limited = jnp.maximum(jnp.minimum(side, jump), 0.0) + jnp.minimum(jnp.maximum(side, jump), 0.0)
    step = factor * limited
    value = jnp.where(upwind, here + step, there - step)
    return speed * value - DIFFUSIVITY * (jump * rlen - slope * gradient)


def vertical_quarter(sums):
    count = len(sums)
    return [0.25 * (sums[min(k + 1, count - 1)] - sums[max(k - 1, 0)]) for k in range(count)]


def kernel(
    temp_hbm, salt_hbm, east_hbm, north_hbm, dx_hbm, dy_hbm, depth_hbm,
    result,
    temp_in, salt_in, east_in, north_in, dx_in, dy_in, depth_in,
    held,
    pack_ts, pack_u, pack_g,
    own_rows, own_speed, own_geo,
    to_east, to_west, to_north, to_south,
    from_west, from_east, from_south, from_north,
    in_sem, send_sem, recv_sem,
):
    lon, lat = lax.axis_index("lon"), lax.axis_index("lat")
    lon_count, lat_count = lax.axis_size("lon"), lax.axis_size("lat")
    west = (lax.rem(lon + lon_count - 1, lon_count), lat)
    east = (lax.rem(lon + 1, lon_count), lat)
    mirror = (lon_count - 1 - lon, lat)
    north = (lon, jnp.minimum(lat + 1, lat_count - 1))
    south = (lon, jnp.maximum(lat - 1, 0))
    top = lat == lat_count - 1
    bottom = lat == 0

    place = lax.rem(lon, 4)
    early = place == 0
    late = jnp.logical_not(early)
    inner = jnp.logical_not(top)
    raised = jnp.logical_not(bottom)
    even = late & (lax.rem(lat, 2) == 0)
    odd_row = late & (lax.rem(lat, 2) == 1)
    leads_east = place >= 2
    leads_west = (place == 1) | (place == 2)
    leads_mirror = top & (place >= 2)
    answers_mirror = top & (place < 2)

    pairs = [(depth_hbm, depth_in)]
    for source, held_in in ((temp_hbm, temp_in), (salt_hbm, salt_in), (east_hbm, east_in)):
        for first in range(0, LEVELS, PIECE):
            part = pl.ds(first, PIECE)
            pairs.append((source.at[part], held_in.at[part]))
    pairs += [(dx_hbm, dx_in), (dy_hbm, dy_in)]
    loads = [pltpu.make_async_copy(a, b, in_sem.at[i]) for i, (a, b) in enumerate(pairs)]
    late_load = pltpu.make_async_copy(north_hbm, north_in, in_sem.at[len(loads)])
    for load in loads:
        load.start()

    barrier = pltpu.get_barrier_semaphore()

    def greet(device):
        pl.semaphore_signal(barrier, inc=1, device_id=device, device_id_type=MESH)

    def greet_if(flag, device):
        @pl.when(flag)
        def _():
            greet(device)

    greet_if(place != 2, east)
    greet_if(early | (place == 3), west)
    greet_if(early & raised, (east[0], south[1]))
    greet_if(early & inner, (east[0], north[1]))
    greet_if(odd_row, south)
    greet_if(odd_row & inner, north)
    greet_if(answers_mirror, mirror)

    def one(flag):
        return jnp.where(flag, 1, 0)

    announced = one(leads_east) + one(leads_west) + one(even) + one(even & raised) + one(leads_mirror)
    announced = announced + one((place == 1) & raised) + one((place == 1) & inner)

    def remote(src, dst, out, into, device):
        return pltpu.make_async_remote_copy(
            src_ref=src, dst_ref=dst, send_sem=send_sem.at[out], recv_sem=recv_sem.at[into],
            device_id=device, device_id_type=MESH,
        )

    def send_east():
        return remote(to_east, from_west, 0, 0, east)

    def send_west():
        return remote(to_west, from_east, 1, 1, west)

    def send_north():
        return remote(to_north, from_south, 2, 2, north)

    def send_mirror():
        return remote(to_north.at[0:32], from_north, 2, 3, mirror)

    def send_south():
        return remote(to_south, from_north, 3, 3, south)

    def start_if(flag, send):
        @pl.when(flag)
        def _():
            send().start()

    for load in loads:
        load.wait()
    late_load.start()

    lane8 = lax.broadcasted_iota(jnp.int32, (8, LANES), 1)
    sub8 = lax.broadcasted_iota(jnp.int32, (8, LANES), 0)
    slot = lane8 & 15
    group = lane8 >> 4

    depth = depth_in[...].astype(F32)
    for k in range(LEVELS):
        wet = depth > float(k)
        held[0, k] = jnp.where(wet, temp_in[k], 0.0)
        held[1, k] = jnp.where(wet, salt_in[k], 0.0)

    def gathered(blocks, base):
        total = turn(blocks[0], base, 1)
        for g in range(1, len(blocks)):
            total = jnp.where(group == g, turn(blocks[g], 16 * g + base, 1), total)
        return total

    def blocks_of(array):
        return [array[8 * r : 8 * r + 8] for r in range(ROWS // 8)]

    dx, dy = dx_in[...], dy_in[...]
    last, first = 1 - LANES, 0
    blocks = [blocks_of(held[0, k]) + blocks_of(held[1, k]) for k in range(LEVELS)]
    blocks_u = [blocks_of(east_in[k]) for k in range(LEVELS)]
    blocks_d, blocks_dx, blocks_dy = blocks_of(depth) * 2, blocks_of(dx), blocks_of(dy)

    def message(near, offset):
        total = gathered(blocks_d, near + 12 + offset)
        total = jnp.where(slot == 14, gathered(blocks_dx, near + 14), total)
        total = jnp.where(slot == 15, gathered(blocks_dy, near + 15), total)
        for k in range(LEVELS):
            total = jnp.where((slot >> 1) == k, gathered(blocks[k], near + 2 * k + offset), total)
        return total

    eastward_u = gathered(blocks_u[0], last)
    for k in range(1, LEVELS):
        eastward_u = jnp.where(slot == k, gathered(blocks_u[k], last + k), eastward_u)
    to_east[0:8] = message(last, 1)
    to_east[8:16] = eastward_u

    @pl.when(late)
    def _():
        pl.semaphore_wait(barrier, announced)

    start_if(leads_east, send_east)

    to_west[...] = message(first, 0)
    start_if(leads_west, send_west)

    late_load.wait()

    for k in range(LEVELS):
        at = 8 * (k // 2) + 2 * (k % 2)
        for tracer in range(2):
            to_north[at + 4 * tracer : at + 4 * tracer + 2] = held[tracer, k, ROWS - 2 : ROWS]
            to_south[at + 4 * tracer : at + 4 * tracer + 2] = held[tracer, k, 0:2]
        to_north[28 + k : 29 + k] = north_in[k, ROWS - 1 : ROWS]
    to_north[24:26] = depth[ROWS - 2 : ROWS]
    to_north[26:27] = dx_in[ROWS - 1 : ROWS]
    to_north[27:28] = dy_in[ROWS - 1 : ROWS]
    to_north[34:40] = jnp.zeros((6, LANES), F32)
    to_south[24:26] = depth[0:2]
    to_south[26:27] = dx_in[0:1]
    to_south[27:28] = dy_in[0:1]
    to_south[28:32] = jnp.zeros((4, LANES), F32)

    @pl.when(top)
    def _():
        for block in range(4):
            x = to_north[8 * block : 8 * block + 8]
            swapped = jnp.where((sub8 & 1) == 0, turn(x, -1, 0), turn(x, 1, 0))
            if block == 3:
                swapped = jnp.where(sub8 < 2, swapped, x)
            to_north[8 * block : 8 * block + 8] = lane_reversed(swapped, lane8)

    @pl.when(bottom)
    def _():
        from_south[...] = jnp.zeros_like(from_south)

    start_if(even, send_north)
    start_if(even & raised, send_south)
    start_if(leads_mirror, send_mirror)

    def opened(blocks):
        x = gathered(blocks, 4)
        return jnp.where(slot < 4, x, turn(x, 4, 1))

    def doubled(x):
        return jnp.where(lane8 < 64, x, turn(x, 64, 1))

    def keep(ref, index, own):
        ref[index] = own
        ref[index + 1] = turn(own, -1, 1)

    for k in range(LEVELS):
        keep(pack_ts, 2 * k, opened(blocks[k]))
        pack_u[k] = opened(blocks_u[k] * 2)
    keep(pack_g, 0, opened(blocks_d))
    keep(pack_g, 2, opened(blocks_dx * 2))
    keep(pack_g, 4, opened(blocks_dy * 2))
    own_depth, own_area = pack_g[0], pack_g[2] * pack_g[4]
    pack_g[6] = jnp.where(slot < 4, own_depth, turn(own_depth, -4, 1))
    pack_g[7] = -TIME_STEP / jnp.where(slot < 4, own_area, turn(own_area, -4, 1))

    lane = lax.broadcasted_iota(jnp.int32, (ROWS, LANES), 1)
    row = lax.broadcasted_iota(jnp.int32, (ROWS, LANES), 0)
    inside_x = (lane >= 1) & (lane <= LANES - 3)
    inside_y = (row >= 1) & (row <= ROWS - 3)
    scale = -TIME_STEP / (dx * dy)

    def axis_part(axis, along, across, inside):
        size = LANES if axis else ROWS
        rlen = 2.0 / (along + turn(along, -1, axis))
        breadth = jnp.where(inside, 0.5 * (across + turn(across, -1, axis)), 0.0)
        least = jnp.minimum(depth, turn(depth, -1, axis))
        return rlen, breadth, least

    geo = [axis_part(1, dx, dy, inside_x), axis_part(0, dy, dx, inside_y)]

    def level_state(k):
        t, s = held[0, k], held[1, k]
        return [(t, s, turn(t, -1, a), turn(s, -1, a)) for a in (1, 0)]

    states = [level_state(k) for k in range(LEVELS)]
    for k in range(LEVELS):
        divergence = [0.0, 0.0]
        for position, axis in enumerate((1, 0)):
            rlen, breadth, least = geo[position]
            t, s, t1, s1 = states[k][position]
            up, down = states[min(k + 1, LEVELS - 1)][position], states[max(k - 1, 0)][position]
            gt = 0.25 * ((up[0] + up[2]) - (down[0] + down[2]))
            gs = 0.25 * ((up[1] + up[3]) - (down[1] + down[3]))
            face = least > float(k)
            jt = jnp.where(face, t1 - t, 0.0)
            js = jnp.where(face, s1 - s, 0.0)
            speed = (east_in if axis else north_in)[k]
            upwind, factor = face_terms(speed, rlen)
            slope = face_slope(CONTRACTION * js - EXPANSION * jt, rlen, CONTRACTION * gs - EXPANSION * gt)
            weight = jnp.where(face, breadth, 0.0)
            for tracer, (a, b, j, g) in enumerate(((t, t1, jt, gt), (s, s1, js, gs))):
                flux = weight * face_flux(
                    a, b, turn(j, 1, axis), j, turn(j, -1, axis), g, slope, speed, upwind, factor, rlen
                )
                divergence[tracer] = divergence[tracer] + (flux - turn(flux, 1, axis))
        wet = depth > float(k)
        for tracer in range(2):
            result[tracer, k] = held[tracer, k] + jnp.where(wet, scale * divergence[tracer], 0.0)

    odd = sub8 & 3
    own_mix = jnp.where(sub8 < 4, -EXPANSION, CONTRACTION)
    other_mix = jnp.where(sub8 < 4, CONTRACTION, -EXPANSION)
    lane_mix = jnp.where(lane8 < 64, -EXPANSION, CONTRACTION)
    lane_other = jnp.where(lane8 < 64, CONTRACTION, -EXPANSION)

    spans = ((2, 4, 29, 31), (1, 2, 0, 1), (2, 4, 30, 32), (0, 2, 0, 2), (2, 3, 31, 32), (0, 2, 1, 3))
    operand_ids = (0, 1, 1, 2, 2, 3)
    for which, (lo, hi, first, last) in zip(operand_ids, spans):
        for tracer in range(2):
            at = 4 * tracer
            for k in range(LEVELS):
                own_rows[which, k, at + lo : at + hi] = held[tracer, k, first:last]
            own_geo[which, at + lo : at + hi] = depth[first:last]
    for tracer in range(2):
        at = 4 * tracer
        for k in range(LEVELS):
            own_speed[k, at + 1 : at + 2] = north_in[k, 0:1]
            own_speed[k, at + 2 : at + 4] = north_in[k, 30:32]
        for which, source in ((4, dx_in), (6, dy_in)):
            own_geo[which, at + 1 : at + 2] = source[0:1]
            own_geo[which, at + 2 : at + 4] = source[30:32]
            own_geo[which + 1, at : at + 2] = source[0:2]
            own_geo[which + 1, at + 2 : at + 3] = source[31:32]
        own_geo[8, at : at + 2] = scale[0:2]
        own_geo[8, at + 2 : at + 4] = scale[30:32]
        own_geo[9, at : at + 2] = depth[0:2]
        own_geo[9, at + 2 : at + 4] = depth[30:32]

    @pl.when(early)
    def _():
        send_west().wait_recv()

    start_if(early & inner, send_north)
    start_if(early & raised, send_south)
    start_if(early, send_east)

    @pl.when(raised)
    def _():
        send_north().wait_recv()

    start_if(odd_row, send_south)
    send_south().wait_recv()
    start_if(odd_row & inner, send_north)
    start_if(answers_mirror, send_mirror)

    def spread(ref, index):
        return jnp.broadcast_to(ref[index : index + 1], (8, LANES))

    depth_a = jnp.where(odd == 0, spread(from_south, 24), jnp.where(odd == 1, spread(from_south, 25), own_geo[0]))
    depth_b = jnp.where(odd == 0, spread(from_south, 25), own_geo[1])
    depth_c = jnp.where(odd == 3, spread(from_north, 24), own_geo[2])
    depth_d = jnp.where(odd == 2, spread(from_north, 24), jnp.where(odd == 3, spread(from_north, 25), own_geo[3]))
    dx_b = jnp.where(odd == 0, spread(from_south, 26), own_geo[4])
    dx_c = jnp.where(odd == 3, spread(from_north, 26), own_geo[5])
    dy_b = jnp.where(odd == 0, spread(from_south, 27), own_geo[6])
    dy_c = jnp.where(odd == 3, spread(from_north, 27), own_geo[7])
    rlen = 2.0 / (dy_b + dy_c)
    breadth = 0.5 * (dx_b + dx_c)
    least_w, least_m, least_e = (
        jnp.minimum(depth_a, depth_b), jnp.minimum(depth_b, depth_c), jnp.minimum(depth_c, depth_d)
    )
    operands = []
    for k in range(LEVELS):
        south = from_south[8 * (k // 2) : 8 * (k // 2) + 8]
        north = from_north[8 * (k // 2) : 8 * (k // 2) + 8]
        south = turn(south, -2 * (k % 2), 0)
        north = turn(north, 2 - 2 * (k % 2), 0)
        operands.append((
            jnp.where(odd < 2, south, own_rows[0, k]),
            jnp.where(odd == 0, turn(south, -1, 0), own_rows[1, k]),
            jnp.where(odd == 3, turn(north, 1, 0), own_rows[2, k]),
            jnp.where(odd >= 2, north, own_rows[3, k]),
        ))
    gradients = vertical_quarter([b + c for _, b, c, _ in operands])
    for k in range(LEVELS):
        a, b, c, d = operands[k]
        jump = jnp.where(least_m > float(k), c - b, 0.0)
        before = jnp.where(least_w > float(k), b - a, 0.0)
        after = jnp.where(least_e > float(k), d - c, 0.0)
        gradient = gradients[k]
        speed = jnp.where(odd == 0, spread(from_south, 28 + k), own_speed[k])
        upwind, factor = face_terms(speed, rlen)
        slope = face_slope(
            own_mix * jump + other_mix * turn(jump, 4, 0), rlen, own_mix * gradient + other_mix * turn(gradient, 4, 0)
        )
        flux = jnp.where(least_m > float(k), breadth, 0.0) * face_flux(
            b, c, before, jump, after, gradient, slope, speed, upwind, factor, rlen
        )
        change = jnp.where(
            odd == 0, turn(flux, -1, 0) - flux,
            jnp.where(odd == 1, -flux, jnp.where(odd == 2, flux, flux - turn(flux, 1, 0))),
        )
        change = jnp.where(own_geo[9] > float(k), own_geo[8] * change, 0.0)
        for tracer in range(2):
            at = 4 * tracer
            result[tracer, k, 0:2] += change[at : at + 2]
            result[tracer, k, ROWS - 2 : ROWS] += change[at + 2 : at + 4]

    @pl.when(early)
    def _():
        pl.semaphore_wait(barrier, 1)

    start_if(early, send_west)

    @pl.when(place == 3)
    def _():
        send_east().wait_recv()

    start_if(place == 3, send_west)

    @pl.when(late)
    def _():
        send_west().wait_recv()

    start_if(place == 1, send_east)

    @pl.when(place != 3)
    def _():
        send_east().wait_recv()

    came_w, came_e = from_west[0:8], from_east[...]
    came_u = doubled(from_west[8:16])
    spread_w, spread_e = doubled(came_w), doubled(came_e)

    def closed(pack, index, low, high, low_from, high_from):
        here = jnp.where((slot >> 1) == 3, turn(low, 6 - low_from, 1), pack[index])
        here = jnp.where((slot >> 1) == 2, turn(high, 4 - high_from, 1), here)
        there = jnp.where(slot == 6, turn(low, 5 - low_from, 1), pack[index + 1])
        there = jnp.where((slot == 3) | (slot == 4), turn(high, 3 - high_from, 1), there)
        return here, there

    depth_here, depth_there = closed(pack_g, 0, came_w, came_e, 12, 12)
    dx_here, dx_there = closed(pack_g, 2, spread_w, spread_e, 13, 14)
    dy_here, dy_there = closed(pack_g, 4, spread_w, spread_e, 14, 15)
    rlen = 2.0 / (dx_here + dx_there)
    edge = (slot == 2) | (slot == 3) | (slot == 7) | (slot == 8)
    breadth = jnp.where(edge, 0.5 * (dy_here + dy_there), 0.0)
    least = jnp.minimum(depth_here, depth_there)
    cell_depth, cell_scale = pack_g[6], pack_g[7]
    values = [closed(pack_ts, 2 * k, came_w, came_e, 2 * k, 2 * k) for k in range(LEVELS)]
    gradients = vertical_quarter([x + y for x, y in values])
    for k in range(LEVELS):
        here, there = values[k]
        face = least > float(k)
        jump = jnp.where(face, there - here, 0.0)
        gradient = gradients[k]
        speed = jnp.where(slot == 7, turn(came_u, 7 - k, 1), pack_u[k])
        upwind, factor = face_terms(speed, rlen)
        slope = face_slope(
            lane_mix * jump + lane_other * turn(jump, 64, 1), rlen,
            lane_mix * gradient + lane_other * turn(gradient, 64, 1),
        )
        flux = jnp.where(face, breadth, 0.0) * face_flux(
            here, there, turn(jump, 1, 1), jump, turn(jump, -1, 1), gradient, slope, speed, upwind, factor, rlen
        )
        change = jnp.where(slot < 4, flux - turn(flux, 1, 1), turn(flux, -4, 1) - turn(flux, -3, 1))
        change = jnp.where(cell_depth > float(k), cell_scale * change, 0.0)
        for tracer in range(2):
            for r in range(ROWS // 8):
                moved = turn(change, 124 - 64 * tracer - 16 * r, 1)
                rows = slice(8 * r, 8 * r + 8)
                result[tracer, k, rows] += jnp.where((lane8 < 2) | (lane8 >= LANES - 2), moved, 0.0)

    send_east().wait_send()
    send_west().wait_send()

    @pl.when(top)
    def _():
        send_mirror().wait_send()

    @pl.when(jnp.logical_not(top))
    def _():
        send_north().wait_send()

    @pl.when(jnp.logical_not(bottom))
    def _():
        send_south().wait_send()


def deliver(result, new_temp, new_salt, sem):
    copies = []
    for tracer, new in enumerate((new_temp, new_salt)):
        for first in range(0, LEVELS, PIECE):
            part = pl.ds(first, PIECE)
            copies.append(pltpu.make_async_copy(result.at[tracer, part], new.at[part], sem.at[len(copies)]))
    for copy in copies:
        copy.start()
    for copy in copies:
        copy.wait()


def local(temp, salt, east, north, dx, dy, depth):
    full = (LEVELS, ROWS, LANES)
    flat = (ROWS, LANES)
    shape = jax.ShapeDtypeStruct(full, F32)
    message = [pltpu.VMEM((rows, LANES), F32) for rows in (16, 8, 40, 32)]
    scratch = [pltpu.VMEM(full, F32)] * 4 + [
        pltpu.VMEM(flat, F32), pltpu.VMEM(flat, F32), pltpu.VMEM(flat, jnp.int32),
        pltpu.VMEM((2,) + full, F32),
        pltpu.VMEM((2 * LEVELS, 8, LANES), F32), pltpu.VMEM((LEVELS, 8, LANES), F32), pltpu.VMEM((8, 8, LANES), F32),
        pltpu.VMEM((4, LEVELS, 8, LANES), F32), pltpu.VMEM((LEVELS, 8, LANES), F32), pltpu.VMEM((10, 8, LANES), F32),
        *message, *message,
        pltpu.SemaphoreType.DMA((3 * (LEVELS // PIECE) + 4,)), pltpu.SemaphoreType.DMA((4,)), pltpu.SemaphoreType.DMA((4,)),
    ]
    inner = pl.BlockSpec(memory_space=pltpu.VMEM)
    result = pl.pallas_call(
        kernel,
        out_shape=pltpu.VMEM((2,) + full, F32),
        in_specs=[pl.BlockSpec(memory_space=pltpu.HBM)] * 7,
        out_specs=inner,
        scratch_shapes=scratch,
        compiler_params=pltpu.CompilerParams(
            collective_id=0, has_side_effects=True, vmem_limit_bytes=16 * 2**20
        ),
        name="tracer_step",
    )(*(pltpu.with_memory_space_constraint(x, pltpu.HBM) for x in (temp, salt, east, north, dx, dy, depth)))
    return pl.pallas_call(
        deliver,
        out_shape=(shape, shape),
        in_specs=[inner],
        out_specs=(pl.BlockSpec(memory_space=pltpu.HBM),) * 2,
        scratch_shapes=[pltpu.SemaphoreType.DMA((2 * LEVELS // PIECE,))],
        name="deliver",
    )(pltpu.with_memory_space_constraint(result, pltpu.VMEM))


def solution(mesh):
    full = P(None, "lat", "lon")
    flat = P("lat", "lon")
    return jax.shard_map(
        local, mesh=mesh, in_specs=(full,) * 4 + (flat,) * 3, out_specs=(full, full), check_vma=False
    )
```

```python
import functools

import jax
import jax.numpy as jnp
from jax import lax
from jax.experimental import pallas as pl
from jax.experimental.pallas import tpu as pltpu
from jax.sharding import PartitionSpec as P

MESH = pl.DeviceIdType.MESH
F32 = jnp.float32

TIME_STEP = 0.2
DIFFUSIVITY = 0.5
EXPANSION = 0.2
CONTRACTION = 0.8
STRAT_FLOOR = 0.5
SLOPE_LIMIT = 2.0

LEVELS = 6
ROWS = 32
LANES = 128
PIECE = 3


def turn(x, shift, axis):
    shift = shift % x.shape[axis]
    return x if shift == 0 else pltpu.roll(x, shift, axis)


def lane_reversed(x, lane):
    for bit in range(7):
        step = 1 << bit
        x = jnp.where((lane & step) == 0, turn(x, -step, 1), turn(x, step, 1))
    return x


def face_terms(speed, rlen):
    return speed >= 0.0, 0.5 - jnp.abs((0.5 * TIME_STEP) * speed * rlen)


def face_slope(rjump, rlen, strat):
    return jnp.clip(rjump * rlen / jnp.maximum(strat, STRAT_FLOOR), -SLOPE_LIMIT, SLOPE_LIMIT)


def face_flux(here, there, before, jump, after, gradient, slope, speed, upwind, factor, rlen):
    side = jnp.where(upwind, before, after)
    limited = jnp.maximum(jnp.minimum(side, jump), 0.0) + jnp.minimum(jnp.maximum(side, jump), 0.0)
    step = factor * limited
    value = jnp.where(upwind, here + step, there - step)
    return speed * value - DIFFUSIVITY * (jump * rlen - slope * gradient)


def vertical_quarter(sums):
    count = len(sums)
    return [0.25 * (sums[min(k + 1, count - 1)] - sums[max(k - 1, 0)]) for k in range(count)]


def fold_east(from_east, pack_ts, pack_g, slot, doubled):
    came = from_east[...]
    spread = doubled(came)
    places = [(pack_ts, 2 * k, came, 2 * k) for k in range(LEVELS)]
    places += [(pack_g, 0, came, 12), (pack_g, 2, spread, 14), (pack_g, 4, spread, 15)]
    for pack, index, message, start in places:
        pack[index] = jnp.where((slot >> 1) == 2, turn(message, 4 - start, 1), pack[index])
        further = (slot == 3) | (slot == 4)
        pack[index + 1] = jnp.where(further, turn(message, 3 - start, 1), pack[index + 1])


def kernel(
    temp_hbm, salt_hbm, east_hbm, north_hbm, dx_hbm, dy_hbm, depth_hbm,
    result, changes,
    temp_in, salt_in, east_in, north_in, dx_in, dy_in, depth_in,
    held,
    pack_ts, pack_u, pack_g,
    own_rows, own_speed, own_geo,
    to_east, to_west, to_north, to_south,
    from_west, from_east, from_south, from_north,
    in_sem, send_sem, recv_sem,
):
    lon, lat = lax.axis_index("lon"), lax.axis_index("lat")
    lon_count, lat_count = lax.axis_size("lon"), lax.axis_size("lat")
    west = (lax.rem(lon + lon_count - 1, lon_count), lat)
    east = (lax.rem(lon + 1, lon_count), lat)
    mirror = (lon_count - 1 - lon, lat)
    north = (lon, jnp.minimum(lat + 1, lat_count - 1))
    south = (lon, jnp.maximum(lat - 1, 0))
    top = lat == lat_count - 1
    bottom = lat == 0

    place = lax.rem(lon, 4)
    early = place == 0
    late = jnp.logical_not(early)
    inner = jnp.logical_not(top)
    raised = jnp.logical_not(bottom)
    even = late & (lax.rem(lat, 2) == 0)
    odd_row = late & (lax.rem(lat, 2) == 1)
    leads_east = place >= 2
    leads_west = (place == 1) | (place == 2)
    leads_mirror = top & (place >= 2)
    answers_mirror = top & (place < 2)

    pairs = [(depth_hbm, depth_in)]
    for source, held_in in ((temp_hbm, temp_in), (salt_hbm, salt_in), (east_hbm, east_in)):
        for first in range(0, LEVELS, PIECE):
            part = pl.ds(first, PIECE)
            pairs.append((source.at[part], held_in.at[part]))
    pairs += [(dx_hbm, dx_in), (dy_hbm, dy_in)]
    loads = [pltpu.make_async_copy(a, b, in_sem.at[i]) for i, (a, b) in enumerate(pairs)]
    late_load = pltpu.make_async_copy(north_hbm, north_in, in_sem.at[len(loads)])
    for load in loads:
        load.start()

    barrier = pltpu.get_barrier_semaphore()

    def greet(device):
        pl.semaphore_signal(barrier, inc=1, device_id=device, device_id_type=MESH)

    def greet_if(flag, device):
        @pl.when(flag)
        def _():
            greet(device)

    greet_if(place != 2, east)
    greet_if(early | (place == 3), west)
    greet_if(early & raised, (east[0], south[1]))
    greet_if(early & inner, (east[0], north[1]))
    greet_if(odd_row, south)
    greet_if(odd_row & inner, north)
    greet_if(answers_mirror, mirror)

    def one(flag):
        return jnp.where(flag, 1, 0)

    announced = one(leads_east) + one(leads_west) + one(even) + one(even & raised) + one(leads_mirror)
    announced = announced + one((place == 1) & raised) + one((place == 1) & inner)

    def remote(src, dst, out, into, device):
        return pltpu.make_async_remote_copy(
            src_ref=src, dst_ref=dst, send_sem=send_sem.at[out], recv_sem=recv_sem.at[into],
            device_id=device, device_id_type=MESH,
        )

    def send_east():
        return remote(to_east, from_west, 0, 0, east)

    def send_west():
        return remote(to_west, from_east, 1, 1, west)

    def send_north():
        return remote(to_north, from_south, 2, 2, north)

    def send_mirror():
        return remote(to_north.at[0:32], from_north, 2, 3, mirror)

    def send_south():
        return remote(to_south, from_north, 3, 3, south)

    def start_if(flag, send):
        @pl.when(flag)
        def _():
            send().start()

    for load in loads:
        load.wait()
    late_load.start()

    lane8 = lax.broadcasted_iota(jnp.int32, (8, LANES), 1)
    sub8 = lax.broadcasted_iota(jnp.int32, (8, LANES), 0)
    slot = lane8 & 15
    group = lane8 >> 4

    depth = depth_in[...].astype(F32)
    for k in range(LEVELS):
        wet = depth > float(k)
        held[0, k] = jnp.where(wet, temp_in[k], 0.0)
        held[1, k] = jnp.where(wet, salt_in[k], 0.0)

    def gathered(blocks, base):
        total = turn(blocks[0], base, 1)
        for g in range(1, len(blocks)):
            total = jnp.where(group == g, turn(blocks[g], 16 * g + base, 1), total)
        return total

    def blocks_of(array):
        return [array[8 * r : 8 * r + 8] for r in range(ROWS // 8)]

    dx, dy = dx_in[...], dy_in[...]
    last, first = 1 - LANES, 0
    blocks = [blocks_of(held[0, k]) + blocks_of(held[1, k]) for k in range(LEVELS)]
    blocks_u = [blocks_of(east_in[k]) for k in range(LEVELS)]
    blocks_d, blocks_dx, blocks_dy = blocks_of(depth) * 2, blocks_of(dx), blocks_of(dy)

    def message(near, offset):
        total = gathered(blocks_d, near + 12 + offset)
        total = jnp.where(slot == 14, gathered(blocks_dx, near + 14), total)
        total = jnp.where(slot == 15, gathered(blocks_dy, near + 15), total)
        for k in range(LEVELS):
            total = jnp.where((slot >> 1) == k, gathered(blocks[k], near + 2 * k + offset), total)
        return total

    eastward_u = gathered(blocks_u[0], last)
    for k in range(1, LEVELS):
        eastward_u = jnp.where(slot == k, gathered(blocks_u[k], last + k), eastward_u)
    to_east[0:8] = message(last, 1)
    to_east[8:16] = eastward_u

    @pl.when(late)
    def _():
        pl.semaphore_wait(barrier, announced)

    start_if(leads_east, send_east)

    to_west[...] = message(first, 0)
    start_if(leads_west, send_west)

    late_load.wait()

    for k in range(LEVELS):
        at = 8 * (k // 2) + 2 * (k % 2)
        for tracer in range(2):
            to_north[at + 4 * tracer : at + 4 * tracer + 2] = held[tracer, k, ROWS - 2 : ROWS]
            to_south[at + 4 * tracer : at + 4 * tracer + 2] = held[tracer, k, 0:2]
        to_north[28 + k : 29 + k] = north_in[k, ROWS - 1 : ROWS]
    to_north[24:26] = depth[ROWS - 2 : ROWS]
    to_north[26:27] = dx_in[ROWS - 1 : ROWS]
    to_north[27:28] = dy_in[ROWS - 1 : ROWS]
    to_north[34:40] = jnp.zeros((6, LANES), F32)
    to_south[24:26] = depth[0:2]
    to_south[26:27] = dx_in[0:1]
    to_south[27:28] = dy_in[0:1]
    to_south[28:32] = jnp.zeros((4, LANES), F32)

    @pl.when(top)
    def _():
        for block in range(4):
            x = to_north[8 * block : 8 * block + 8]
            swapped = jnp.where((sub8 & 1) == 0, turn(x, -1, 0), turn(x, 1, 0))
            if block == 3:
                swapped = jnp.where(sub8 < 2, swapped, x)
            to_north[8 * block : 8 * block + 8] = lane_reversed(swapped, lane8)

    @pl.when(bottom)
    def _():
        from_south[...] = jnp.zeros_like(from_south)

    start_if(even, send_north)
    start_if(even & raised, send_south)
    start_if(leads_mirror, send_mirror)

    def opened(blocks):
        x = gathered(blocks, 4)
        return jnp.where(slot < 4, x, turn(x, 4, 1))

    def doubled(x):
        return jnp.where(lane8 < 64, x, turn(x, 64, 1))

    def keep(ref, index, own):
        ref[index] = own
        ref[index + 1] = turn(own, -1, 1)

    for k in range(LEVELS):
        keep(pack_ts, 2 * k, opened(blocks[k]))
        pack_u[k] = opened(blocks_u[k] * 2)
    keep(pack_g, 0, opened(blocks_d))
    keep(pack_g, 2, opened(blocks_dx * 2))
    keep(pack_g, 4, opened(blocks_dy * 2))
    own_depth, own_area = pack_g[0], pack_g[2] * pack_g[4]
    pack_g[6] = jnp.where(slot < 4, own_depth, turn(own_depth, -4, 1))
    pack_g[7] = -TIME_STEP / jnp.where(slot < 4, own_area, turn(own_area, -4, 1))

    lane = lax.broadcasted_iota(jnp.int32, (ROWS, LANES), 1)
    row = lax.broadcasted_iota(jnp.int32, (ROWS, LANES), 0)
    inside_x = (lane >= 1) & (lane <= LANES - 3)
    inside_y = (row >= 1) & (row <= ROWS - 3)
    scale = -TIME_STEP / (dx * dy)

    def axis_part(axis, along, across, inside):
        size = LANES if axis else ROWS
        rlen = 2.0 / (along + turn(along, -1, axis))
        breadth = jnp.where(inside, 0.5 * (across + turn(across, -1, axis)), 0.0)
        least = jnp.minimum(depth, turn(depth, -1, axis))
        return rlen, breadth, least

    geo = [axis_part(1, dx, dy, inside_x), axis_part(0, dy, dx, inside_y)]

    def level_state(k):
        t, s = held[0, k], held[1, k]
        return [(t, s, turn(t, -1, a), turn(s, -1, a)) for a in (1, 0)]

    states = [level_state(k) for k in range(LEVELS)]
    for k in range(LEVELS):
        divergence = [0.0, 0.0]
        for position, axis in enumerate((1, 0)):
            rlen, breadth, least = geo[position]
            t, s, t1, s1 = states[k][position]
            up, down = states[min(k + 1, LEVELS - 1)][position], states[max(k - 1, 0)][position]
            gt = 0.25 * ((up[0] + up[2]) - (down[0] + down[2]))
            gs = 0.25 * ((up[1] + up[3]) - (down[1] + down[3]))
            face = least > float(k)
            jt = jnp.where(face, t1 - t, 0.0)
            js = jnp.where(face, s1 - s, 0.0)
            speed = (east_in if axis else north_in)[k]
            upwind, factor = face_terms(speed, rlen)
            slope = face_slope(CONTRACTION * js - EXPANSION * jt, rlen, CONTRACTION * gs - EXPANSION * gt)
            weight = jnp.where(face, breadth, 0.0)
            for tracer, (a, b, j, g) in enumerate(((t, t1, jt, gt), (s, s1, js, gs))):
                flux = weight * face_flux(
                    a, b, turn(j, 1, axis), j, turn(j, -1, axis), g, slope, speed, upwind, factor, rlen
                )
                divergence[tracer] = divergence[tracer] + (flux - turn(flux, 1, axis))
        wet = depth > float(k)
        for tracer in range(2):
            result[tracer, k] = held[tracer, k] + jnp.where(wet, scale * divergence[tracer], 0.0)

    odd = sub8 & 3
    own_mix = jnp.where(sub8 < 4, -EXPANSION, CONTRACTION)
    other_mix = jnp.where(sub8 < 4, CONTRACTION, -EXPANSION)
    lane_mix = jnp.where(lane8 < 64, -EXPANSION, CONTRACTION)
    lane_other = jnp.where(lane8 < 64, CONTRACTION, -EXPANSION)

    spans = ((2, 4, 29, 31), (1, 2, 0, 1), (2, 4, 30, 32), (0, 2, 0, 2), (2, 3, 31, 32), (0, 2, 1, 3))
    operand_ids = (0, 1, 1, 2, 2, 3)
    for which, (lo, hi, first, last) in zip(operand_ids, spans):
        for tracer in range(2):
            at = 4 * tracer
            for k in range(LEVELS):
                own_rows[which, k, at + lo : at + hi] = held[tracer, k, first:last]
            own_geo[which, at + lo : at + hi] = depth[first:last]
    for tracer in range(2):
        at = 4 * tracer
        for k in range(LEVELS):
            own_speed[k, at + 1 : at + 2] = north_in[k, 0:1]
            own_speed[k, at + 2 : at + 4] = north_in[k, 30:32]
        for which, source in ((4, dx_in), (6, dy_in)):
            own_geo[which, at + 1 : at + 2] = source[0:1]
            own_geo[which, at + 2 : at + 4] = source[30:32]
            own_geo[which + 1, at : at + 2] = source[0:2]
            own_geo[which + 1, at + 2 : at + 3] = source[31:32]
        own_geo[8, at : at + 2] = scale[0:2]
        own_geo[8, at + 2 : at + 4] = scale[30:32]
        own_geo[9, at : at + 2] = depth[0:2]
        own_geo[9, at + 2 : at + 4] = depth[30:32]

    @pl.when(early)
    def _():
        send_west().wait_recv()

    start_if(early & inner, send_north)
    start_if(early & raised, send_south)
    start_if(early, send_east)
    eastern_halo = functools.partial(fold_east, from_east, pack_ts, pack_g, slot, doubled)
    pl.when(early)(eastern_halo)

    @pl.when(raised)
    def _():
        send_north().wait_recv()

    start_if(odd_row, send_south)
    send_south().wait_recv()
    start_if(odd_row & inner, send_north)
    start_if(answers_mirror, send_mirror)

    def spread(ref, index):
        return jnp.broadcast_to(ref[index : index + 1], (8, LANES))

    depth_a = jnp.where(odd == 0, spread(from_south, 24), jnp.where(odd == 1, spread(from_south, 25), own_geo[0]))
    depth_b = jnp.where(odd == 0, spread(from_south, 25), own_geo[1])
    depth_c = jnp.where(odd == 3, spread(from_north, 24), own_geo[2])
    depth_d = jnp.where(odd == 2, spread(from_north, 24), jnp.where(odd == 3, spread(from_north, 25), own_geo[3]))
    dx_b = jnp.where(odd == 0, spread(from_south, 26), own_geo[4])
    dx_c = jnp.where(odd == 3, spread(from_north, 26), own_geo[5])
    dy_b = jnp.where(odd == 0, spread(from_south, 27), own_geo[6])
    dy_c = jnp.where(odd == 3, spread(from_north, 27), own_geo[7])
    rlen = 2.0 / (dy_b + dy_c)
    breadth = 0.5 * (dx_b + dx_c)
    least_w, least_m, least_e = (
        jnp.minimum(depth_a, depth_b), jnp.minimum(depth_b, depth_c), jnp.minimum(depth_c, depth_d)
    )
    operands = []
    for k in range(LEVELS):
        south = from_south[8 * (k // 2) : 8 * (k // 2) + 8]
        north = from_north[8 * (k // 2) : 8 * (k // 2) + 8]
        south = turn(south, -2 * (k % 2), 0)
        north = turn(north, 2 - 2 * (k % 2), 0)
        operands.append((
            jnp.where(odd < 2, south, own_rows[0, k]),
            jnp.where(odd == 0, turn(south, -1, 0), own_rows[1, k]),
            jnp.where(odd == 3, turn(north, 1, 0), own_rows[2, k]),
            jnp.where(odd >= 2, north, own_rows[3, k]),
        ))
    gradients = vertical_quarter([b + c for _, b, c, _ in operands])
    for k in range(LEVELS):
        a, b, c, d = operands[k]
        jump = jnp.where(least_m > float(k), c - b, 0.0)
        before = jnp.where(least_w > float(k), b - a, 0.0)
        after = jnp.where(least_e > float(k), d - c, 0.0)
        gradient = gradients[k]
        speed = jnp.where(odd == 0, spread(from_south, 28 + k), own_speed[k])
        upwind, factor = face_terms(speed, rlen)
        slope = face_slope(
            own_mix * jump + other_mix * turn(jump, 4, 0), rlen, own_mix * gradient + other_mix * turn(gradient, 4, 0)
        )
        flux = jnp.where(least_m > float(k), breadth, 0.0) * face_flux(
            b, c, before, jump, after, gradient, slope, speed, upwind, factor, rlen
        )
        change = jnp.where(
            odd == 0, turn(flux, -1, 0) - flux,
            jnp.where(odd == 1, -flux, jnp.where(odd == 2, flux, flux - turn(flux, 1, 0))),
        )
        change = jnp.where(own_geo[9] > float(k), own_geo[8] * change, 0.0)
        for tracer in range(2):
            at = 4 * tracer
            result[tracer, k, 0:2] += change[at : at + 2]
            result[tracer, k, ROWS - 2 : ROWS] += change[at + 2 : at + 4]

    @pl.when(early)
    def _():
        pl.semaphore_wait(barrier, 1)

    start_if(early, send_west)

    @pl.when(place == 3)
    def _():
        send_east().wait_recv()

    start_if(place == 3, send_west)

    @pl.when(late)
    def _():
        send_west().wait_recv()

    start_if(place == 1, send_east)

    @pl.when(place != 3)
    def _():
        send_east().wait_recv()

    pl.when(late)(eastern_halo)
    came_w = from_west[0:8]
    came_u = doubled(from_west[8:16])
    spread_w = doubled(came_w)

    def closed(pack, index, low, start):
        here = jnp.where((slot >> 1) == 3, turn(low, 6 - start, 1), pack[index])
        return here, jnp.where(slot == 6, turn(low, 5 - start, 1), pack[index + 1])

    depth_here, depth_there = closed(pack_g, 0, came_w, 12)
    dx_here, dx_there = closed(pack_g, 2, spread_w, 13)
    dy_here, dy_there = closed(pack_g, 4, spread_w, 14)
    rlen = 2.0 / (dx_here + dx_there)
    edge = (slot == 2) | (slot == 3) | (slot == 7) | (slot == 8)
    breadth = jnp.where(edge, 0.5 * (dy_here + dy_there), 0.0)
    least = jnp.minimum(depth_here, depth_there)
    cell_depth, cell_scale = pack_g[6], pack_g[7]
    values = [closed(pack_ts, 2 * k, came_w, 2 * k) for k in range(LEVELS)]
    gradients = vertical_quarter([x + y for x, y in values])
    for k in range(LEVELS):
        here, there = values[k]
        face = least > float(k)
        jump = jnp.where(face, there - here, 0.0)
        gradient = gradients[k]
        speed = jnp.where(slot == 7, turn(came_u, 7 - k, 1), pack_u[k])
        upwind, factor = face_terms(speed, rlen)
        slope = face_slope(
            lane_mix * jump + lane_other * turn(jump, 64, 1), rlen,
            lane_mix * gradient + lane_other * turn(gradient, 64, 1),
        )
        flux = jnp.where(face, breadth, 0.0) * face_flux(
            here, there, turn(jump, 1, 1), jump, turn(jump, -1, 1), gradient, slope, speed, upwind, factor, rlen
        )
        change = jnp.where(slot < 4, flux - turn(flux, 1, 1), turn(flux, -4, 1) - turn(flux, -3, 1))
        change = jnp.where(cell_depth > float(k), cell_scale * change, 0.0)
        changes[k] = change

    send_east().wait_send()
    send_west().wait_send()

    @pl.when(top)
    def _():
        send_mirror().wait_send()

    @pl.when(jnp.logical_not(top))
    def _():
        send_north().wait_send()

    @pl.when(jnp.logical_not(bottom))
    def _():
        send_south().wait_send()


def deliver(result, changes, new_temp, new_salt, patched, sem):
    lane = lax.broadcasted_iota(jnp.int32, (8, LANES), 1)
    edge = (lane < 2) | (lane >= LANES - 2)
    copies = []
    for first in range(0, LEVELS, PIECE):
        for tracer, new in enumerate((new_temp, new_salt)):
            for k in range(first, first + PIECE):
                for r in range(ROWS // 8):
                    moved = turn(changes[k], 124 - 64 * tracer - 16 * r, 1)
                    rows = slice(8 * r, 8 * r + 8)
                    patched[tracer, k, rows] = result[tracer, k, rows] + jnp.where(edge, moved, 0.0)
            part = pl.ds(first, PIECE)
            copies.append(pltpu.make_async_copy(patched.at[tracer, part], new.at[part], sem.at[len(copies)]))
            copies[-1].start()
    for copy in copies:
        copy.wait()


def local(temp, salt, east, north, dx, dy, depth):
    full = (LEVELS, ROWS, LANES)
    flat = (ROWS, LANES)
    shape = jax.ShapeDtypeStruct(full, F32)
    message = [pltpu.VMEM((rows, LANES), F32) for rows in (16, 8, 40, 32)]
    scratch = [pltpu.VMEM(full, F32)] * 4 + [
        pltpu.VMEM(flat, F32), pltpu.VMEM(flat, F32), pltpu.VMEM(flat, jnp.int32),
        pltpu.VMEM((2,) + full, F32),
        pltpu.VMEM((2 * LEVELS, 8, LANES), F32), pltpu.VMEM((LEVELS, 8, LANES), F32), pltpu.VMEM((8, 8, LANES), F32),
        pltpu.VMEM((4, LEVELS, 8, LANES), F32), pltpu.VMEM((LEVELS, 8, LANES), F32), pltpu.VMEM((10, 8, LANES), F32),
        *message, *message,
        pltpu.SemaphoreType.DMA((3 * (LEVELS // PIECE) + 4,)), pltpu.SemaphoreType.DMA((4,)), pltpu.SemaphoreType.DMA((4,)),
    ]
    inner = pl.BlockSpec(memory_space=pltpu.VMEM)
    result, changes = pl.pallas_call(
        kernel,
        out_shape=(pltpu.VMEM((2,) + full, F32), pltpu.VMEM((LEVELS, 8, LANES), F32)),
        in_specs=[pl.BlockSpec(memory_space=pltpu.HBM)] * 7,
        out_specs=(inner, inner),
        scratch_shapes=scratch,
        compiler_params=pltpu.CompilerParams(
            collective_id=0, has_side_effects=True, vmem_limit_bytes=16 * 2**20
        ),
        name="tracer_step",
    )(*(pltpu.with_memory_space_constraint(x, pltpu.HBM) for x in (temp, salt, east, north, dx, dy, depth)))
    return pl.pallas_call(
        deliver,
        out_shape=(shape, shape),
        in_specs=[inner, inner],
        out_specs=(pl.BlockSpec(memory_space=pltpu.HBM),) * 2,
        scratch_shapes=[pltpu.VMEM((2,) + full, F32), pltpu.SemaphoreType.DMA((2 * LEVELS // PIECE,))],
        name="deliver",
    )(*(pltpu.with_memory_space_constraint(x, pltpu.VMEM) for x in (result, changes)))


def solution(mesh):
    full = P(None, "lat", "lon")
    flat = P("lat", "lon")
    return jax.shard_map(
        local, mesh=mesh, in_specs=(full,) * 4 + (flat,) * 3, out_specs=(full, full), check_vma=False
    )
```

```python
import functools

import jax
import jax.numpy as jnp
from jax import lax
from jax.experimental import pallas as pl
from jax.experimental.pallas import tpu as pltpu
from jax.sharding import PartitionSpec as P

MESH = pl.DeviceIdType.MESH
F32 = jnp.float32

TIME_STEP = 0.2
DIFFUSIVITY = 0.5
EXPANSION = 0.2
CONTRACTION = 0.8
STRAT_FLOOR = 0.5
SLOPE_LIMIT = 2.0

LEVELS = 6
ROWS = 32
LANES = 128
PIECE = 3


def turn(x, shift, axis):
    shift = shift % x.shape[axis]
    return x if shift == 0 else pltpu.roll(x, shift, axis)


def lane_reversed(x, lane):
    for bit in range(7):
        step = 1 << bit
        x = jnp.where((lane & step) == 0, turn(x, -step, 1), turn(x, step, 1))
    return x


def face_terms(speed, rlen):
    return speed >= 0.0, 0.5 - jnp.abs((0.5 * TIME_STEP) * speed * rlen)


def face_slope(rjump, rlen, strat):
    return jnp.clip(rjump * rlen / jnp.maximum(strat, STRAT_FLOOR), -SLOPE_LIMIT, SLOPE_LIMIT)


def face_flux(here, there, before, jump, after, gradient, slope, speed, upwind, factor, rlen):
    side = jnp.where(upwind, before, after)
    limited = jnp.maximum(jnp.minimum(side, jump), 0.0) + jnp.minimum(jnp.maximum(side, jump), 0.0)
    step = factor * limited
    value = jnp.where(upwind, here + step, there - step)
    return speed * value - DIFFUSIVITY * (jump * rlen - slope * gradient)


def vertical_quarter(sums):
    count = len(sums)
    return [0.25 * (sums[min(k + 1, count - 1)] - sums[max(k - 1, 0)]) for k in range(count)]


def fold_east(from_east, pack_ts, pack_g, slot, doubled):
    came = from_east[...]
    spread = doubled(came)
    places = [(pack_ts, 2 * k, came, 2 * k) for k in range(LEVELS)]
    places += [(pack_g, 0, came, 12), (pack_g, 2, spread, 14), (pack_g, 4, spread, 15)]
    for pack, index, message, start in places:
        pack[index] = jnp.where((slot >> 1) == 2, turn(message, 4 - start, 1), pack[index])
        further = (slot == 3) | (slot == 4)
        pack[index + 1] = jnp.where(further, turn(message, 3 - start, 1), pack[index + 1])


def kernel(
    temp_hbm, salt_hbm, east_hbm, north_hbm, dx_hbm, dy_hbm, depth_hbm,
    result, changes,
    temp_in, salt_in, east_in, north_in, dx_in, dy_in, depth_in,
    held, west_in,
    pack_ts, pack_u, pack_g,
    own_rows, own_speed, own_geo,
    to_east, to_west, to_north, to_south,
    from_west, from_east, from_south, from_north,
    in_sem, send_sem, recv_sem,
):
    lon, lat = lax.axis_index("lon"), lax.axis_index("lat")
    lon_count, lat_count = lax.axis_size("lon"), lax.axis_size("lat")
    west = (lax.rem(lon + lon_count - 1, lon_count), lat)
    east = (lax.rem(lon + 1, lon_count), lat)
    mirror = (lon_count - 1 - lon, lat)
    north = (lon, jnp.minimum(lat + 1, lat_count - 1))
    south = (lon, jnp.maximum(lat - 1, 0))
    top = lat == lat_count - 1
    bottom = lat == 0

    place = lax.rem(lon, 4)
    early = place == 0
    late = jnp.logical_not(early)
    inner = jnp.logical_not(top)
    raised = jnp.logical_not(bottom)
    even = late & (lax.rem(lat, 2) == 0)
    odd_row = late & (lax.rem(lat, 2) == 1)
    leads_east = place >= 2
    leads_west = (place == 1) | (place == 2)
    leads_mirror = top & (place >= 2)
    answers_mirror = top & (place < 2)

    pairs = [(depth_hbm, depth_in)]
    for source, held_in in ((temp_hbm, temp_in), (salt_hbm, salt_in), (east_hbm, east_in)):
        for first in range(0, LEVELS, PIECE):
            part = pl.ds(first, PIECE)
            pairs.append((source.at[part], held_in.at[part]))
    pairs += [(dx_hbm, dx_in), (dy_hbm, dy_in)]
    loads = [pltpu.make_async_copy(a, b, in_sem.at[i]) for i, (a, b) in enumerate(pairs)]
    late_load = pltpu.make_async_copy(north_hbm, north_in, in_sem.at[len(loads)])
    for load in loads:
        load.start()

    barrier = pltpu.get_barrier_semaphore()

    def greet(device):
        pl.semaphore_signal(barrier, inc=1, device_id=device, device_id_type=MESH)

    def greet_if(flag, device):
        @pl.when(flag)
        def _():
            greet(device)

    greet_if(place != 2, east)
    greet_if(early | (place == 3), west)
    greet_if(early & raised, (east[0], south[1]))
    greet_if(early & inner, (east[0], north[1]))
    greet_if(odd_row, south)
    greet_if(odd_row & inner, north)
    greet_if(answers_mirror, mirror)

    def one(flag):
        return jnp.where(flag, 1, 0)

    announced = one(leads_east) + one(leads_west) + one(even) + one(even & raised) + one(leads_mirror)
    announced = announced + one((place == 1) & raised) + one((place == 1) & inner)

    def remote(src, dst, out, into, device):
        return pltpu.make_async_remote_copy(
            src_ref=src, dst_ref=dst, send_sem=send_sem.at[out], recv_sem=recv_sem.at[into],
            device_id=device, device_id_type=MESH,
        )

    def send_east():
        return remote(to_east, from_west, 0, 0, east)

    def send_west():
        return remote(to_west, from_east, 1, 1, west)

    def send_north():
        return remote(to_north, from_south, 2, 2, north)

    def send_mirror():
        return remote(to_north.at[0:32], from_north, 2, 3, mirror)

    def send_south():
        return remote(to_south, from_north, 3, 3, south)

    def start_if(flag, send):
        @pl.when(flag)
        def _():
            send().start()

    for load in loads:
        load.wait()
    late_load.start()

    lane8 = lax.broadcasted_iota(jnp.int32, (8, LANES), 1)
    sub8 = lax.broadcasted_iota(jnp.int32, (8, LANES), 0)
    slot = lane8 & 15
    group = lane8 >> 4

    depth = depth_in[...].astype(F32)
    for k in range(LEVELS):
        wet = depth > float(k)
        held[0, k] = jnp.where(wet, temp_in[k], 0.0)
        held[1, k] = jnp.where(wet, salt_in[k], 0.0)

    def gathered(blocks, base):
        total = turn(blocks[0], base, 1)
        for g in range(1, len(blocks)):
            total = jnp.where(group == g, turn(blocks[g], 16 * g + base, 1), total)
        return total

    def blocks_of(array):
        return [array[8 * r : 8 * r + 8] for r in range(ROWS // 8)]

    dx, dy = dx_in[...], dy_in[...]
    last, first = 1 - LANES, 0
    blocks = [blocks_of(held[0, k]) + blocks_of(held[1, k]) for k in range(LEVELS)]
    blocks_u = [blocks_of(east_in[k]) for k in range(LEVELS)]
    blocks_d, blocks_dx, blocks_dy = blocks_of(depth) * 2, blocks_of(dx), blocks_of(dy)

    def message(near, offset):
        total = gathered(blocks_d, near + 12 + offset)
        total = jnp.where(slot == 14, gathered(blocks_dx, near + 14), total)
        total = jnp.where(slot == 15, gathered(blocks_dy, near + 15), total)
        for k in range(LEVELS):
            total = jnp.where((slot >> 1) == k, gathered(blocks[k], near + 2 * k + offset), total)
        return total

    eastward_u = gathered(blocks_u[0], last)
    for k in range(1, LEVELS):
        eastward_u = jnp.where(slot == k, gathered(blocks_u[k], last + k), eastward_u)
    to_east[0:8] = message(last, 1)
    to_east[8:16] = eastward_u

    @pl.when(late)
    def _():
        pl.semaphore_wait(barrier, announced)

    start_if(leads_east, send_east)

    to_west[...] = message(first, 0)
    start_if(leads_west, send_west)

    late_load.wait()

    for k in range(LEVELS):
        at = 8 * (k // 2) + 2 * (k % 2)
        for tracer in range(2):
            to_north[at + 4 * tracer : at + 4 * tracer + 2] = held[tracer, k, ROWS - 2 : ROWS]
            to_south[at + 4 * tracer : at + 4 * tracer + 2] = held[tracer, k, 0:2]
        to_north[28 + k : 29 + k] = north_in[k, ROWS - 1 : ROWS]
    to_north[24:26] = depth[ROWS - 2 : ROWS]
    to_north[26:27] = dx_in[ROWS - 1 : ROWS]
    to_north[27:28] = dy_in[ROWS - 1 : ROWS]
    to_north[34:40] = jnp.zeros((6, LANES), F32)
    to_south[24:26] = depth[0:2]
    to_south[26:27] = dx_in[0:1]
    to_south[27:28] = dy_in[0:1]
    to_south[28:32] = jnp.zeros((4, LANES), F32)

    @pl.when(top)
    def _():
        for block in range(4):
            x = to_north[8 * block : 8 * block + 8]
            swapped = jnp.where((sub8 & 1) == 0, turn(x, -1, 0), turn(x, 1, 0))
            if block == 3:
                swapped = jnp.where(sub8 < 2, swapped, x)
            to_north[8 * block : 8 * block + 8] = lane_reversed(swapped, lane8)

    @pl.when(bottom)
    def _():
        from_south[...] = jnp.zeros_like(from_south)

    start_if(even, send_north)
    start_if(even & raised, send_south)
    start_if(leads_mirror, send_mirror)

    def opened(blocks):
        x = gathered(blocks, 4)
        return jnp.where(slot < 4, x, turn(x, 4, 1))

    def doubled(x):
        return jnp.where(lane8 < 64, x, turn(x, 64, 1))

    def keep(ref, index, own):
        ref[index] = own
        ref[index + 1] = turn(own, -1, 1)

    for k in range(LEVELS):
        keep(pack_ts, 2 * k, opened(blocks[k]))
        pack_u[k] = opened(blocks_u[k] * 2)
    keep(pack_g, 0, opened(blocks_d))
    keep(pack_g, 2, opened(blocks_dx * 2))
    keep(pack_g, 4, opened(blocks_dy * 2))
    own_depth, own_area = pack_g[0], pack_g[2] * pack_g[4]
    pack_g[6] = jnp.where(slot < 4, own_depth, turn(own_depth, -4, 1))
    pack_g[7] = -TIME_STEP / jnp.where(slot < 4, own_area, turn(own_area, -4, 1))

    lane = lax.broadcasted_iota(jnp.int32, (ROWS, LANES), 1)
    row = lax.broadcasted_iota(jnp.int32, (ROWS, LANES), 0)
    inside_x = (lane >= 1) & (lane <= LANES - 3)
    inside_y = (row >= 1) & (row <= ROWS - 3)
    scale = -TIME_STEP / (dx * dy)

    def axis_part(axis, along, across, inside):
        size = LANES if axis else ROWS
        rlen = 2.0 / (along + turn(along, -1, axis))
        breadth = jnp.where(inside, 0.5 * (across + turn(across, -1, axis)), 0.0)
        least = jnp.minimum(depth, turn(depth, -1, axis))
        return rlen, breadth, least

    geo = [axis_part(1, dx, dy, inside_x), axis_part(0, dy, dx, inside_y)]

    def level_state(k):
        t, s = held[0, k], held[1, k]
        return [(t, s, turn(t, -1, a), turn(s, -1, a)) for a in (1, 0)]

    states = [level_state(k) for k in range(LEVELS)]
    for k in range(LEVELS):
        divergence = [0.0, 0.0]
        for position, axis in enumerate((1, 0)):
            rlen, breadth, least = geo[position]
            t, s, t1, s1 = states[k][position]
            up, down = states[min(k + 1, LEVELS - 1)][position], states[max(k - 1, 0)][position]
            gt = 0.25 * ((up[0] + up[2]) - (down[0] + down[2]))
            gs = 0.25 * ((up[1] + up[3]) - (down[1] + down[3]))
            face = least > float(k)
            jt = jnp.where(face, t1 - t, 0.0)
            js = jnp.where(face, s1 - s, 0.0)
            speed = (east_in if axis else north_in)[k]
            upwind, factor = face_terms(speed, rlen)
            slope = face_slope(CONTRACTION * js - EXPANSION * jt, rlen, CONTRACTION * gs - EXPANSION * gt)
            weight = jnp.where(face, breadth, 0.0)
            for tracer, (a, b, j, g) in enumerate(((t, t1, jt, gt), (s, s1, js, gs))):
                flux = weight * face_flux(
                    a, b, turn(j, 1, axis), j, turn(j, -1, axis), g, slope, speed, upwind, factor, rlen
                )
                divergence[tracer] = divergence[tracer] + (flux - turn(flux, 1, axis))
        wet = depth > float(k)
        for tracer in range(2):
            result[tracer, k] = held[tracer, k] + jnp.where(wet, scale * divergence[tracer], 0.0)

    odd = sub8 & 3
    own_mix = jnp.where(sub8 < 4, -EXPANSION, CONTRACTION)
    other_mix = jnp.where(sub8 < 4, CONTRACTION, -EXPANSION)
    lane_mix = jnp.where(lane8 < 64, -EXPANSION, CONTRACTION)
    lane_other = jnp.where(lane8 < 64, CONTRACTION, -EXPANSION)

    spans = ((2, 4, 29, 31), (1, 2, 0, 1), (2, 4, 30, 32), (0, 2, 0, 2), (2, 3, 31, 32), (0, 2, 1, 3))
    operand_ids = (0, 1, 1, 2, 2, 3)
    for which, (lo, hi, first, last) in zip(operand_ids, spans):
        for tracer in range(2):
            at = 4 * tracer
            for k in range(LEVELS):
                own_rows[which, k, at + lo : at + hi] = held[tracer, k, first:last]
            own_geo[which, at + lo : at + hi] = depth[first:last]
    for tracer in range(2):
        at = 4 * tracer
        for k in range(LEVELS):
            own_speed[k, at + 1 : at + 2] = north_in[k, 0:1]
            own_speed[k, at + 2 : at + 4] = north_in[k, 30:32]
        for which, source in ((4, dx_in), (6, dy_in)):
            own_geo[which, at + 1 : at + 2] = source[0:1]
            own_geo[which, at + 2 : at + 4] = source[30:32]
            own_geo[which + 1, at : at + 2] = source[0:2]
            own_geo[which + 1, at + 2 : at + 3] = source[31:32]
        own_geo[8, at : at + 2] = scale[0:2]
        own_geo[8, at + 2 : at + 4] = scale[30:32]
        own_geo[9, at : at + 2] = depth[0:2]
        own_geo[9, at + 2 : at + 4] = depth[30:32]

    @pl.when(early)
    def _():
        send_west().wait_recv()

    start_if(early & inner, send_north)
    start_if(early & raised, send_south)
    start_if(early, send_east)
    eastern_halo = functools.partial(fold_east, from_east, pack_ts, pack_g, slot, doubled)
    pl.when(early)(eastern_halo)

    @pl.when(raised)
    def _():
        send_north().wait_recv()

    start_if(odd_row, send_south)
    send_south().wait_recv()
    start_if(odd_row & inner, send_north)
    start_if(answers_mirror, send_mirror)

    def spread(ref, index):
        return jnp.broadcast_to(ref[index : index + 1], (8, LANES))

    depth_a = jnp.where(odd == 0, spread(from_south, 24), jnp.where(odd == 1, spread(from_south, 25), own_geo[0]))
    depth_b = jnp.where(odd == 0, spread(from_south, 25), own_geo[1])
    depth_c = jnp.where(odd == 3, spread(from_north, 24), own_geo[2])
    depth_d = jnp.where(odd == 2, spread(from_north, 24), jnp.where(odd == 3, spread(from_north, 25), own_geo[3]))
    dx_b = jnp.where(odd == 0, spread(from_south, 26), own_geo[4])
    dx_c = jnp.where(odd == 3, spread(from_north, 26), own_geo[5])
    dy_b = jnp.where(odd == 0, spread(from_south, 27), own_geo[6])
    dy_c = jnp.where(odd == 3, spread(from_north, 27), own_geo[7])
    rlen = 2.0 / (dy_b + dy_c)
    breadth = 0.5 * (dx_b + dx_c)
    least_w, least_m, least_e = (
        jnp.minimum(depth_a, depth_b), jnp.minimum(depth_b, depth_c), jnp.minimum(depth_c, depth_d)
    )
    operands = []
    for k in range(LEVELS):
        south = from_south[8 * (k // 2) : 8 * (k // 2) + 8]
        north = from_north[8 * (k // 2) : 8 * (k // 2) + 8]
        south = turn(south, -2 * (k % 2), 0)
        north = turn(north, 2 - 2 * (k % 2), 0)
        operands.append((
            jnp.where(odd < 2, south, own_rows[0, k]),
            jnp.where(odd == 0, turn(south, -1, 0), own_rows[1, k]),
            jnp.where(odd == 3, turn(north, 1, 0), own_rows[2, k]),
            jnp.where(odd >= 2, north, own_rows[3, k]),
        ))
    gradients = vertical_quarter([b + c for _, b, c, _ in operands])
    for k in range(LEVELS):
        a, b, c, d = operands[k]
        jump = jnp.where(least_m > float(k), c - b, 0.0)
        before = jnp.where(least_w > float(k), b - a, 0.0)
        after = jnp.where(least_e > float(k), d - c, 0.0)
        gradient = gradients[k]
        speed = jnp.where(odd == 0, spread(from_south, 28 + k), own_speed[k])
        upwind, factor = face_terms(speed, rlen)
        slope = face_slope(
            own_mix * jump + other_mix * turn(jump, 4, 0), rlen, own_mix * gradient + other_mix * turn(gradient, 4, 0)
        )
        flux = jnp.where(least_m > float(k), breadth, 0.0) * face_flux(
            b, c, before, jump, after, gradient, slope, speed, upwind, factor, rlen
        )
        change = jnp.where(
            odd == 0, turn(flux, -1, 0) - flux,
            jnp.where(odd == 1, -flux, jnp.where(odd == 2, flux, flux - turn(flux, 1, 0))),
        )
        change = jnp.where(own_geo[9] > float(k), own_geo[8] * change, 0.0)
        for tracer in range(2):
            at = 4 * tracer
            result[tracer, k, 0:2] += change[at : at + 2]
            result[tracer, k, ROWS - 2 : ROWS] += change[at + 2 : at + 4]

    west_in[...] = to_east[...]

    @pl.loop(0, 2)
    def _(attempt):
        @pl.when(attempt == 1)
        def _():
            @pl.when(early)
            def _():
                pl.semaphore_wait(barrier, 1)

            start_if(early, send_west)

            @pl.when(place == 3)
            def _():
                send_east().wait_recv()

            start_if(place == 3, send_west)

            @pl.when(late)
            def _():
                send_west().wait_recv()

            start_if(place == 1, send_east)

            @pl.when(place != 3)
            def _():
                send_east().wait_recv()

            pl.when(late)(eastern_halo)
            west_in[...] = from_west[...]

        came_w = west_in[0:8]
        came_u = doubled(west_in[8:16])
        spread_w = doubled(came_w)

        def closed(pack, index, low, start):
            here = jnp.where((slot >> 1) == 3, turn(low, 6 - start, 1), pack[index])
            return here, jnp.where(slot == 6, turn(low, 5 - start, 1), pack[index + 1])

        depth_here, depth_there = closed(pack_g, 0, came_w, 12)
        dx_here, dx_there = closed(pack_g, 2, spread_w, 13)
        dy_here, dy_there = closed(pack_g, 4, spread_w, 14)
        rlen = 2.0 / (dx_here + dx_there)
        edge = (slot == 2) | (slot == 3) | (slot == 7) | (slot == 8)
        breadth = jnp.where(edge, 0.5 * (dy_here + dy_there), 0.0)
        least = jnp.minimum(depth_here, depth_there)
        cell_depth, cell_scale = pack_g[6], pack_g[7]
        values = [closed(pack_ts, 2 * k, came_w, 2 * k) for k in range(LEVELS)]
        gradients = vertical_quarter([x + y for x, y in values])
        for k in range(LEVELS):
            here, there = values[k]
            face = least > float(k)
            jump = jnp.where(face, there - here, 0.0)
            gradient = gradients[k]
            speed = jnp.where(slot == 7, turn(came_u, 7 - k, 1), pack_u[k])
            upwind, factor = face_terms(speed, rlen)
            slope = face_slope(
                lane_mix * jump + lane_other * turn(jump, 64, 1), rlen,
                lane_mix * gradient + lane_other * turn(gradient, 64, 1),
            )
            flux = jnp.where(face, breadth, 0.0) * face_flux(
                here, there, turn(jump, 1, 1), jump, turn(jump, -1, 1), gradient, slope, speed, upwind, factor, rlen
            )
            change = jnp.where(slot < 4, flux - turn(flux, 1, 1), turn(flux, -4, 1) - turn(flux, -3, 1))
            change = jnp.where(cell_depth > float(k), cell_scale * change, 0.0)
            changes[k] = change

    send_east().wait_send()
    send_west().wait_send()

    @pl.when(top)
    def _():
        send_mirror().wait_send()

    @pl.when(jnp.logical_not(top))
    def _():
        send_north().wait_send()

    @pl.when(jnp.logical_not(bottom))
    def _():
        send_south().wait_send()


def deliver(result, changes, new_temp, new_salt, patched, sem):
    lane = lax.broadcasted_iota(jnp.int32, (8, LANES), 1)
    edge = (lane < 2) | (lane >= LANES - 2)
    copies = []
    for first in range(0, LEVELS, PIECE):
        for tracer, new in enumerate((new_temp, new_salt)):
            for k in range(first, first + PIECE):
                for r in range(ROWS // 8):
                    moved = turn(changes[k], 124 - 64 * tracer - 16 * r, 1)
                    rows = slice(8 * r, 8 * r + 8)
                    patched[tracer, k, rows] = result[tracer, k, rows] + jnp.where(edge, moved, 0.0)
            part = pl.ds(first, PIECE)
            copies.append(pltpu.make_async_copy(patched.at[tracer, part], new.at[part], sem.at[len(copies)]))
            copies[-1].start()
    for copy in copies:
        copy.wait()


def local(temp, salt, east, north, dx, dy, depth):
    full = (LEVELS, ROWS, LANES)
    flat = (ROWS, LANES)
    shape = jax.ShapeDtypeStruct(full, F32)
    message = [pltpu.VMEM((rows, LANES), F32) for rows in (16, 8, 40, 32)]
    scratch = [pltpu.VMEM(full, F32)] * 4 + [
        pltpu.VMEM(flat, F32), pltpu.VMEM(flat, F32), pltpu.VMEM(flat, jnp.int32),
        pltpu.VMEM((2,) + full, F32), pltpu.VMEM((16, LANES), F32),
        pltpu.VMEM((2 * LEVELS, 8, LANES), F32), pltpu.VMEM((LEVELS, 8, LANES), F32), pltpu.VMEM((8, 8, LANES), F32),
        pltpu.VMEM((4, LEVELS, 8, LANES), F32), pltpu.VMEM((LEVELS, 8, LANES), F32), pltpu.VMEM((10, 8, LANES), F32),
        *message, *message,
        pltpu.SemaphoreType.DMA((3 * (LEVELS // PIECE) + 4,)), pltpu.SemaphoreType.DMA((4,)), pltpu.SemaphoreType.DMA((4,)),
    ]
    inner = pl.BlockSpec(memory_space=pltpu.VMEM)
    result, changes = pl.pallas_call(
        kernel,
        out_shape=(pltpu.VMEM((2,) + full, F32), pltpu.VMEM((LEVELS, 8, LANES), F32)),
        in_specs=[pl.BlockSpec(memory_space=pltpu.HBM)] * 7,
        out_specs=(inner, inner),
        scratch_shapes=scratch,
        compiler_params=pltpu.CompilerParams(
            collective_id=0, has_side_effects=True, vmem_limit_bytes=16 * 2**20
        ),
        name="tracer_step",
    )(*(pltpu.with_memory_space_constraint(x, pltpu.HBM) for x in (temp, salt, east, north, dx, dy, depth)))
    return pl.pallas_call(
        deliver,
        out_shape=(shape, shape),
        in_specs=[inner, inner],
        out_specs=(pl.BlockSpec(memory_space=pltpu.HBM),) * 2,
        scratch_shapes=[pltpu.VMEM((2,) + full, F32), pltpu.SemaphoreType.DMA((2 * LEVELS // PIECE,))],
        name="deliver",
    )(*(pltpu.with_memory_space_constraint(x, pltpu.VMEM) for x in (result, changes)))


def solution(mesh):
    full = P(None, "lat", "lon")
    flat = P("lat", "lon")
    return jax.shard_map(
        local, mesh=mesh, in_specs=(full,) * 4 + (flat,) * 3, out_specs=(full, full), check_vma=False
    )
```

```python
import functools

import jax
import jax.numpy as jnp
from jax import lax
from jax.experimental import pallas as pl
from jax.experimental.pallas import tpu as pltpu
from jax.sharding import PartitionSpec as P

MESH = pl.DeviceIdType.MESH
F32 = jnp.float32

TIME_STEP = 0.2
DIFFUSIVITY = 0.5
EXPANSION = 0.2
CONTRACTION = 0.8
STRAT_FLOOR = 0.5
SLOPE_LIMIT = 2.0

LEVELS = 6
ROWS = 32
LANES = 128
PIECE = 3


def turn(x, shift, axis):
    shift = shift % x.shape[axis]
    return x if shift == 0 else pltpu.roll(x, shift, axis)


def lane_reversed(x, lane):
    for bit in range(7):
        step = 1 << bit
        x = jnp.where((lane & step) == 0, turn(x, -step, 1), turn(x, step, 1))
    return x


def face_terms(speed, rlen):
    return speed >= 0.0, 0.5 - jnp.abs((0.5 * TIME_STEP) * speed * rlen)


def face_slope(rjump, rlen, strat):
    return jnp.clip(rjump * rlen / jnp.maximum(strat, STRAT_FLOOR), -SLOPE_LIMIT, SLOPE_LIMIT)


def face_flux(here, there, before, jump, after, gradient, slope, speed, upwind, factor, rlen):
    side = jnp.where(upwind, before, after)
    limited = jnp.maximum(jnp.minimum(side, jump), 0.0) + jnp.minimum(jnp.maximum(side, jump), 0.0)
    step = factor * limited
    value = jnp.where(upwind, here + step, there - step)
    return speed * value - DIFFUSIVITY * (jump * rlen - slope * gradient)


def vertical_quarter(sums):
    count = len(sums)
    return [0.25 * (sums[min(k + 1, count - 1)] - sums[max(k - 1, 0)]) for k in range(count)]


def fold_east(from_east, pack_ts, pack_g, slot, doubled):
    came = from_east[...]
    spread = doubled(came)
    places = [(pack_ts, 2 * k, came, 2 * k) for k in range(LEVELS)]
    places += [(pack_g, 0, came, 12), (pack_g, 2, spread, 14), (pack_g, 4, spread, 15)]
    for pack, index, message, start in places:
        pack[index] = jnp.where((slot >> 1) == 2, turn(message, 4 - start, 1), pack[index])
        further = (slot == 3) | (slot == 4)
        pack[index + 1] = jnp.where(further, turn(message, 3 - start, 1), pack[index + 1])


def kernel(
    temp_hbm, salt_hbm, east_hbm, north_hbm, dx_hbm, dy_hbm, depth_hbm,
    result, changes,
    fields, north_in, depth_in,
    held, west_in,
    pack_ts, pack_u, pack_g,
    own_rows, own_speed, own_geo,
    to_east, to_west, to_north, to_south,
    from_west, from_east, from_south, from_north,
    in_sem, send_sem, recv_sem,
):
    lon, lat = lax.axis_index("lon"), lax.axis_index("lat")
    lon_count, lat_count = lax.axis_size("lon"), lax.axis_size("lat")
    west = (lax.rem(lon + lon_count - 1, lon_count), lat)
    east = (lax.rem(lon + 1, lon_count), lat)
    mirror = (lon_count - 1 - lon, lat)
    north = (lon, jnp.minimum(lat + 1, lat_count - 1))
    south = (lon, jnp.maximum(lat - 1, 0))
    top = lat == lat_count - 1
    bottom = lat == 0

    place = lax.rem(lon, 4)
    early = place == 0
    late = jnp.logical_not(early)
    inner = jnp.logical_not(top)
    raised = jnp.logical_not(bottom)
    even = late & (lax.rem(lat, 2) == 0)
    odd_row = late & (lax.rem(lat, 2) == 1)
    leads_east = place >= 2
    leads_west = (place == 1) | (place == 2)
    leads_mirror = top & (place >= 2)
    answers_mirror = top & (place < 2)

    temp_in, salt_in, east_in = (fields.at[pl.ds(first, LEVELS)] for first in range(0, 3 * LEVELS, LEVELS))
    dx_in, dy_in = fields.at[3 * LEVELS], fields.at[3 * LEVELS + 1]
    pairs = [(depth_hbm, depth_in)]
    for source, held_in in ((temp_hbm, temp_in), (salt_hbm, salt_in), (east_hbm, east_in)):
        for first in range(0, LEVELS, PIECE):
            part = pl.ds(first, PIECE)
            pairs.append((source.at[part], held_in.at[part]))
    pairs += [(dx_hbm, dx_in), (dy_hbm, dy_in)]
    loads = [pltpu.make_async_copy(a, b, in_sem.at[min(i, 1)]) for i, (a, b) in enumerate(pairs)]
    late_load = pltpu.make_async_copy(north_hbm, north_in, in_sem.at[2])
    for load in loads:
        load.start()

    barrier = pltpu.get_barrier_semaphore()

    def greet(device):
        pl.semaphore_signal(barrier, inc=1, device_id=device, device_id_type=MESH)

    def greet_if(flag, device):
        @pl.when(flag)
        def _():
            greet(device)

    greet_if(place != 2, east)
    greet_if(early | (place == 3), west)
    greet_if(early & raised, (east[0], south[1]))
    greet_if(early & inner, (east[0], north[1]))
    greet_if(odd_row, south)
    greet_if(odd_row & inner, north)
    greet_if(answers_mirror, mirror)

    def one(flag):
        return jnp.where(flag, 1, 0)

    announced = one(leads_east) + one(leads_west) + one(even) + one(even & raised) + one(leads_mirror)
    announced = announced + one((place == 1) & raised) + one((place == 1) & inner)

    def remote(src, dst, out, into, device):
        return pltpu.make_async_remote_copy(
            src_ref=src, dst_ref=dst, send_sem=send_sem.at[out], recv_sem=recv_sem.at[into],
            device_id=device, device_id_type=MESH,
        )

    def send_east():
        return remote(to_east, from_west, 0, 0, east)

    def send_west():
        return remote(to_west, from_east, 1, 1, west)

    def send_north():
        return remote(to_north, from_south, 2, 2, north)

    def send_mirror():
        return remote(to_north.at[0:32], from_north, 2, 3, mirror)

    def send_south():
        return remote(to_south, from_north, 3, 3, south)

    def start_if(flag, send):
        @pl.when(flag)
        def _():
            send().start()

    loads[0].wait()
    pltpu.make_async_copy(fields, fields, in_sem.at[1]).wait()
    late_load.start()

    lane8 = lax.broadcasted_iota(jnp.int32, (8, LANES), 1)
    sub8 = lax.broadcasted_iota(jnp.int32, (8, LANES), 0)
    slot = lane8 & 15
    group = lane8 >> 4

    depth = depth_in[...].astype(F32)
    for k in range(LEVELS):
        wet = depth > float(k)
        held[0, k] = jnp.where(wet, temp_in[k], 0.0)
        held[1, k] = jnp.where(wet, salt_in[k], 0.0)

    def gathered(blocks, base):
        total = turn(blocks[0], base, 1)
        for g in range(1, len(blocks)):
            total = jnp.where(group == g, turn(blocks[g], 16 * g + base, 1), total)
        return total

    def blocks_of(array):
        return [array[8 * r : 8 * r + 8] for r in range(ROWS // 8)]

    dx, dy = dx_in[...], dy_in[...]
    last, first = 1 - LANES, 0
    blocks = [blocks_of(held[0, k]) + blocks_of(held[1, k]) for k in range(LEVELS)]
    blocks_u = [blocks_of(east_in[k]) for k in range(LEVELS)]
    blocks_d, blocks_dx, blocks_dy = blocks_of(depth) * 2, blocks_of(dx), blocks_of(dy)

    def message(near, offset):
        total = gathered(blocks_d, near + 12 + offset)
        total = jnp.where(slot == 14, gathered(blocks_dx, near + 14), total)
        total = jnp.where(slot == 15, gathered(blocks_dy, near + 15), total)
        for k in range(LEVELS):
            total = jnp.where((slot >> 1) == k, gathered(blocks[k], near + 2 * k + offset), total)
        return total

    eastward_u = gathered(blocks_u[0], last)
    for k in range(1, LEVELS):
        eastward_u = jnp.where(slot == k, gathered(blocks_u[k], last + k), eastward_u)
    to_east[0:8] = message(last, 1)
    to_east[8:16] = eastward_u

    @pl.when(late)
    def _():
        pl.semaphore_wait(barrier, announced)

    start_if(leads_east, send_east)

    to_west[...] = message(first, 0)
    start_if(leads_west, send_west)

    late_load.wait()

    for k in range(LEVELS):
        at = 8 * (k // 2) + 2 * (k % 2)
        for tracer in range(2):
            to_north[at + 4 * tracer : at + 4 * tracer + 2] = held[tracer, k, ROWS - 2 : ROWS]
            to_south[at + 4 * tracer : at + 4 * tracer + 2] = held[tracer, k, 0:2]
        to_north[28 + k : 29 + k] = north_in[k, ROWS - 1 : ROWS]
    to_north[24:26] = depth[ROWS - 2 : ROWS]
    to_north[26:27] = dx_in[ROWS - 1 : ROWS]
    to_north[27:28] = dy_in[ROWS - 1 : ROWS]
    to_north[34:40] = jnp.zeros((6, LANES), F32)
    to_south[24:26] = depth[0:2]
    to_south[26:27] = dx_in[0:1]
    to_south[27:28] = dy_in[0:1]
    to_south[28:32] = jnp.zeros((4, LANES), F32)

    @pl.when(top)
    def _():
        for block in range(4):
            x = to_north[8 * block : 8 * block + 8]
            swapped = jnp.where((sub8 & 1) == 0, turn(x, -1, 0), turn(x, 1, 0))
            if block == 3:
                swapped = jnp.where(sub8 < 2, swapped, x)
            to_north[8 * block : 8 * block + 8] = lane_reversed(swapped, lane8)

    @pl.when(bottom)
    def _():
        from_south[...] = jnp.zeros_like(from_south)

    start_if(even, send_north)
    start_if(even & raised, send_south)
    start_if(leads_mirror, send_mirror)

    def opened(blocks):
        x = gathered(blocks, 4)
        return jnp.where(slot < 4, x, turn(x, 4, 1))

    def doubled(x):
        return jnp.where(lane8 < 64, x, turn(x, 64, 1))

    def keep(ref, index, own):
        ref[index] = own
        ref[index + 1] = turn(own, -1, 1)

    for k in range(LEVELS):
        keep(pack_ts, 2 * k, opened(blocks[k]))
        pack_u[k] = opened(blocks_u[k] * 2)
    keep(pack_g, 0, opened(blocks_d))
    keep(pack_g, 2, opened(blocks_dx * 2))
    keep(pack_g, 4, opened(blocks_dy * 2))
    own_depth, own_area = pack_g[0], pack_g[2] * pack_g[4]
    pack_g[6] = jnp.where(slot < 4, own_depth, turn(own_depth, -4, 1))
    pack_g[7] = -TIME_STEP / jnp.where(slot < 4, own_area, turn(own_area, -4, 1))

    lane = lax.broadcasted_iota(jnp.int32, (ROWS, LANES), 1)
    row = lax.broadcasted_iota(jnp.int32, (ROWS, LANES), 0)
    inside_x = (lane >= 1) & (lane <= LANES - 3)
    inside_y = (row >= 1) & (row <= ROWS - 3)
    scale = -TIME_STEP / (dx * dy)

    def axis_part(axis, along, across, inside):
        size = LANES if axis else ROWS
        rlen = 2.0 / (along + turn(along, -1, axis))
        breadth = jnp.where(inside, 0.5 * (across + turn(across, -1, axis)), 0.0)
        least = jnp.minimum(depth, turn(depth, -1, axis))
        return rlen, breadth, least

    geo = [axis_part(1, dx, dy, inside_x), axis_part(0, dy, dx, inside_y)]

    def level_state(k):
        t, s = held[0, k], held[1, k]
        return [(t, s, turn(t, -1, a), turn(s, -1, a)) for a in (1, 0)]

    states = [level_state(k) for k in range(LEVELS)]
    for k in range(LEVELS):
        divergence = [0.0, 0.0]
        for position, axis in enumerate((1, 0)):
            rlen, breadth, least = geo[position]
            t, s, t1, s1 = states[k][position]
            up, down = states[min(k + 1, LEVELS - 1)][position], states[max(k - 1, 0)][position]
            gt = 0.25 * ((up[0] + up[2]) - (down[0] + down[2]))
            gs = 0.25 * ((up[1] + up[3]) - (down[1] + down[3]))
            face = least > float(k)
            jt = jnp.where(face, t1 - t, 0.0)
            js = jnp.where(face, s1 - s, 0.0)
            speed = (east_in if axis else north_in)[k]
            upwind, factor = face_terms(speed, rlen)
            slope = face_slope(CONTRACTION * js - EXPANSION * jt, rlen, CONTRACTION * gs - EXPANSION * gt)
            weight = jnp.where(face, breadth, 0.0)
            for tracer, (a, b, j, g) in enumerate(((t, t1, jt, gt), (s, s1, js, gs))):
                flux = weight * face_flux(
                    a, b, turn(j, 1, axis), j, turn(j, -1, axis), g, slope, speed, upwind, factor, rlen
                )
                divergence[tracer] = divergence[tracer] + (flux - turn(flux, 1, axis))
        wet = depth > float(k)
        for tracer in range(2):
            result[tracer, k] = held[tracer, k] + jnp.where(wet, scale * divergence[tracer], 0.0)

    odd = sub8 & 3
    own_mix = jnp.where(sub8 < 4, -EXPANSION, CONTRACTION)
    other_mix = jnp.where(sub8 < 4, CONTRACTION, -EXPANSION)
    lane_mix = jnp.where(lane8 < 64, -EXPANSION, CONTRACTION)
    lane_other = jnp.where(lane8 < 64, CONTRACTION, -EXPANSION)

    spans = ((2, 4, 29, 31), (1, 2, 0, 1), (2, 4, 30, 32), (0, 2, 0, 2), (2, 3, 31, 32), (0, 2, 1, 3))
    operand_ids = (0, 1, 1, 2, 2, 3)
    for which, (lo, hi, first, last) in zip(operand_ids, spans):
        for tracer in range(2):
            at = 4 * tracer
            for k in range(LEVELS):
                own_rows[which, k, at + lo : at + hi] = held[tracer, k, first:last]
            own_geo[which, at + lo : at + hi] = depth[first:last]
    for tracer in range(2):
        at = 4 * tracer
        for k in range(LEVELS):
            own_speed[k, at + 1 : at + 2] = north_in[k, 0:1]
            own_speed[k, at + 2 : at + 4] = north_in[k, 30:32]
        for which, source in ((4, dx_in), (6, dy_in)):
            own_geo[which, at + 1 : at + 2] = source[0:1]
            own_geo[which, at + 2 : at + 4] = source[30:32]
            own_geo[which + 1, at : at + 2] = source[0:2]
            own_geo[which + 1, at + 2 : at + 3] = source[31:32]
        own_geo[8, at : at + 2] = scale[0:2]
        own_geo[8, at + 2 : at + 4] = scale[30:32]
        own_geo[9, at : at + 2] = depth[0:2]
        own_geo[9, at + 2 : at + 4] = depth[30:32]

    @pl.when(early)
    def _():
        send_west().wait_recv()

    start_if(early & inner, send_north)
    start_if(early & raised, send_south)
    start_if(early, send_east)
    eastern_halo = functools.partial(fold_east, from_east, pack_ts, pack_g, slot, doubled)
    pl.when(early)(eastern_halo)

    @pl.when(raised)
    def _():
        send_north().wait_recv()

    start_if(odd_row, send_south)
    send_south().wait_recv()
    start_if(odd_row & inner, send_north)
    start_if(answers_mirror, send_mirror)

    def spread(ref, index):
        return jnp.broadcast_to(ref[index : index + 1], (8, LANES))

    depth_a = jnp.where(odd == 0, spread(from_south, 24), jnp.where(odd == 1, spread(from_south, 25), own_geo[0]))
    depth_b = jnp.where(odd == 0, spread(from_south, 25), own_geo[1])
    depth_c = jnp.where(odd == 3, spread(from_north, 24), own_geo[2])
    depth_d = jnp.where(odd == 2, spread(from_north, 24), jnp.where(odd == 3, spread(from_north, 25), own_geo[3]))
    dx_b = jnp.where(odd == 0, spread(from_south, 26), own_geo[4])
    dx_c = jnp.where(odd == 3, spread(from_north, 26), own_geo[5])
    dy_b = jnp.where(odd == 0, spread(from_south, 27), own_geo[6])
    dy_c = jnp.where(odd == 3, spread(from_north, 27), own_geo[7])
    rlen = 2.0 / (dy_b + dy_c)
    breadth = 0.5 * (dx_b + dx_c)
    least_w, least_m, least_e = (
        jnp.minimum(depth_a, depth_b), jnp.minimum(depth_b, depth_c), jnp.minimum(depth_c, depth_d)
    )
    operands = []
    for k in range(LEVELS):
        south = from_south[8 * (k // 2) : 8 * (k // 2) + 8]
        north = from_north[8 * (k // 2) : 8 * (k // 2) + 8]
        south = turn(south, -2 * (k % 2), 0)
        north = turn(north, 2 - 2 * (k % 2), 0)
        operands.append((
            jnp.where(odd < 2, south, own_rows[0, k]),
            jnp.where(odd == 0, turn(south, -1, 0), own_rows[1, k]),
            jnp.where(odd == 3, turn(north, 1, 0), own_rows[2, k]),
            jnp.where(odd >= 2, north, own_rows[3, k]),
        ))
    gradients = vertical_quarter([b + c for _, b, c, _ in operands])
    for k in range(LEVELS):
        a, b, c, d = operands[k]
        jump = jnp.where(least_m > float(k), c - b, 0.0)
        before = jnp.where(least_w > float(k), b - a, 0.0)
        after = jnp.where(least_e > float(k), d - c, 0.0)
        gradient = gradients[k]
        speed = jnp.where(odd == 0, spread(from_south, 28 + k), own_speed[k])
        upwind, factor = face_terms(speed, rlen)
        slope = face_slope(
            own_mix * jump + other_mix * turn(jump, 4, 0), rlen, own_mix * gradient + other_mix * turn(gradient, 4, 0)
        )
        flux = jnp.where(least_m > float(k), breadth, 0.0) * face_flux(
            b, c, before, jump, after, gradient, slope, speed, upwind, factor, rlen
        )
        change = jnp.where(
            odd == 0, turn(flux, -1, 0) - flux,
            jnp.where(odd == 1, -flux, jnp.where(odd == 2, flux, flux - turn(flux, 1, 0))),
        )
        change = jnp.where(own_geo[9] > float(k), own_geo[8] * change, 0.0)
        for tracer in range(2):
            at = 4 * tracer
            result[tracer, k, 0:2] += change[at : at + 2]
            result[tracer, k, ROWS - 2 : ROWS] += change[at + 2 : at + 4]

    west_in[...] = to_east[...]

    @pl.loop(0, 2)
    def _(attempt):
        @pl.when(attempt == 1)
        def _():
            @pl.when(early)
            def _():
                pl.semaphore_wait(barrier, 1)

            start_if(early, send_west)

            @pl.when(place == 3)
            def _():
                send_east().wait_recv()

            start_if(place == 3, send_west)

            @pl.when(late)
            def _():
                send_west().wait_recv()

            start_if(place == 1, send_east)

            @pl.when(place != 3)
            def _():
                send_east().wait_recv()

            pl.when(late)(eastern_halo)
            west_in[...] = from_west[...]

        came_w = west_in[0:8]
        came_u = doubled(west_in[8:16])
        spread_w = doubled(came_w)

        def closed(pack, index, low, start):
            here = jnp.where((slot >> 1) == 3, turn(low, 6 - start, 1), pack[index])
            return here, jnp.where(slot == 6, turn(low, 5 - start, 1), pack[index + 1])

        depth_here, depth_there = closed(pack_g, 0, came_w, 12)
        dx_here, dx_there = closed(pack_g, 2, spread_w, 13)
        dy_here, dy_there = closed(pack_g, 4, spread_w, 14)
        rlen = 2.0 / (dx_here + dx_there)
        edge = (slot == 2) | (slot == 3) | (slot == 7) | (slot == 8)
        breadth = jnp.where(edge, 0.5 * (dy_here + dy_there), 0.0)
        least = jnp.minimum(depth_here, depth_there)
        cell_depth, cell_scale = pack_g[6], pack_g[7]
        values = [closed(pack_ts, 2 * k, came_w, 2 * k) for k in range(LEVELS)]
        gradients = vertical_quarter([x + y for x, y in values])
        for k in range(LEVELS):
            here, there = values[k]
            face = least > float(k)
            jump = jnp.where(face, there - here, 0.0)
            gradient = gradients[k]
            speed = jnp.where(slot == 7, turn(came_u, 7 - k, 1), pack_u[k])
            upwind, factor = face_terms(speed, rlen)
            slope = face_slope(
                lane_mix * jump + lane_other * turn(jump, 64, 1), rlen,
                lane_mix * gradient + lane_other * turn(gradient, 64, 1),
            )
            flux = jnp.where(face, breadth, 0.0) * face_flux(
                here, there, turn(jump, 1, 1), jump, turn(jump, -1, 1), gradient, slope, speed, upwind, factor, rlen
            )
            change = jnp.where(slot < 4, flux - turn(flux, 1, 1), turn(flux, -4, 1) - turn(flux, -3, 1))
            change = jnp.where(cell_depth > float(k), cell_scale * change, 0.0)
            changes[k] = change

    send_east().wait_send()
    send_west().wait_send()

    @pl.when(top)
    def _():
        send_mirror().wait_send()

    @pl.when(jnp.logical_not(top))
    def _():
        send_north().wait_send()

    @pl.when(jnp.logical_not(bottom))
    def _():
        send_south().wait_send()


def deliver(result, changes, new_temp, new_salt, patched, sem):
    lane = lax.broadcasted_iota(jnp.int32, (8, LANES), 1)
    edge = (lane < 2) | (lane >= LANES - 2)
    copies = []
    for first in range(0, LEVELS, PIECE):
        for tracer, new in enumerate((new_temp, new_salt)):
            for k in range(first, first + PIECE):
                for r in range(ROWS // 8):
                    moved = turn(changes[k], 124 - 64 * tracer - 16 * r, 1)
                    rows = slice(8 * r, 8 * r + 8)
                    patched[tracer, k, rows] = result[tracer, k, rows] + jnp.where(edge, moved, 0.0)
            part = pl.ds(first, PIECE)
            copies.append(pltpu.make_async_copy(patched.at[tracer, part], new.at[part], sem.at[len(copies)]))
            copies[-1].start()
    for copy in copies:
        copy.wait()


def local(temp, salt, east, north, dx, dy, depth):
    full = (LEVELS, ROWS, LANES)
    flat = (ROWS, LANES)
    shape = jax.ShapeDtypeStruct(full, F32)
    message = [pltpu.VMEM((rows, LANES), F32) for rows in (16, 8, 40, 32)]
    scratch = [
        pltpu.VMEM((3 * LEVELS + 2,) + flat, F32), pltpu.VMEM(full, F32), pltpu.VMEM(flat, jnp.int32),
        pltpu.VMEM((2,) + full, F32), pltpu.VMEM((16, LANES), F32),
        pltpu.VMEM((2 * LEVELS, 8, LANES), F32), pltpu.VMEM((LEVELS, 8, LANES), F32), pltpu.VMEM((8, 8, LANES), F32),
        pltpu.VMEM((4, LEVELS, 8, LANES), F32), pltpu.VMEM((LEVELS, 8, LANES), F32), pltpu.VMEM((10, 8, LANES), F32),
        *message, *message,
        pltpu.SemaphoreType.DMA((3,)), pltpu.SemaphoreType.DMA((4,)), pltpu.SemaphoreType.DMA((4,)),
    ]
    inner = pl.BlockSpec(memory_space=pltpu.VMEM)
    result, changes = pl.pallas_call(
        kernel,
        out_shape=(pltpu.VMEM((2,) + full, F32), pltpu.VMEM((LEVELS, 8, LANES), F32)),
        in_specs=[pl.BlockSpec(memory_space=pltpu.HBM)] * 7,
        out_specs=(inner, inner),
        scratch_shapes=scratch,
        compiler_params=pltpu.CompilerParams(
            collective_id=0, has_side_effects=True, vmem_limit_bytes=16 * 2**20
        ),
        name="tracer_step",
    )(*(pltpu.with_memory_space_constraint(x, pltpu.HBM) for x in (temp, salt, east, north, dx, dy, depth)))
    return pl.pallas_call(
        deliver,
        out_shape=(shape, shape),
        in_specs=[inner, inner],
        out_specs=(pl.BlockSpec(memory_space=pltpu.HBM),) * 2,
        scratch_shapes=[pltpu.VMEM((2,) + full, F32), pltpu.SemaphoreType.DMA((2 * LEVELS // PIECE,))],
        name="deliver",
    )(*(pltpu.with_memory_space_constraint(x, pltpu.VMEM) for x in (result, changes)))


def solution(mesh):
    full = P(None, "lat", "lon")
    flat = P("lat", "lon")
    return jax.shard_map(
        local, mesh=mesh, in_specs=(full,) * 4 + (flat,) * 3, out_specs=(full, full), check_vma=False
    )
```
